32 devices in a mesh: seq: 4 (over y, core), exp: 8 (over z, x).
Axes of the slice: x: 2, y: 2, z: 4, core: 2. Of those that a mesh axis runs over, the one named last changes fastest.
Arguments:
- resid: bfloat16 [8, 512, 4096], P('exp', 'seq'), may hold values from -1.5 to 1.5
- queries: bfloat16 [8, 512, 4096], P('exp', 'seq'), may hold values from -8 to 8
- span_rotated_keys: bfloat16 [8, 512, 512], P('exp', 'seq'), may hold values from -6 to 6
- span_value_rows: bfloat16 [8, 512, 512], P('exp', 'seq'), may hold values from -6 to 6
- key_cache: bfloat16 [8, 4, 256, 128], P('exp', None, 'seq'), may hold values from -8 to 8
- prefix_value_cache: bfloat16 [8, 4, 256, 128], P('exp', None, 'seq'), may hold values from -6 to 6
- prefix_len: int32 [8], P('exp'), may hold values from 1 to 256, as said below
- out_weight: bfloat16 [4096, 4096], P('seq'), may hold values from -0.09375 to 0.09375
- norm_gain: float32 [4096], replicated, may hold values from 0.1 to 1.9
- router_weight: bfloat16 [4096, 32], replicated
- expert_ids: int32 [8, 512, 8], P('exp', 'seq'), may hold values from 0 to 31, all different within a row; in each aligned block of 128 rows (0 to 127, 128 to 255, ..., all dimensions but the last counted through in order) at most 36 rows name the same one
- w_gate: bfloat16 [32, 4096, 768], P(('seq', 'exp')), may hold values from -0.09375 to 0.09375
- w_up: bfloat16 [32, 4096, 768], P(('seq', 'exp')), may hold values from -0.09375 to 0.09375
- w_down: bfloat16 [32, 768, 4096], P(('seq', 'exp')), may hold values from -0.21875 to 0.21875
Outputs:
- layer_out: bfloat16 [8, 512, 4096], P('exp', 'seq')
The draws below stay inside these ranges and needn't reach their ends.
Inputs may be any that keep to these rules, and one draw needn't show every extreme that they name: `expert_ids`: in the 128 consecutive tokens of one index of seq, no expert is named by more than 36 routes, a bound that some block reaches. `prefix_len`: some prompt's prefix fills the cache.
All inputs are finite; a program needn't handle non-finite values.
Results may differ from the reference program's by a relative error of at most 0.03.
Values may be sent and summed in bfloat16 or wider, within the bound.
A program may use at most 192 MiB of HBM per device.

```python
import math
import jax
import jax.numpy as jnp
import numpy as np
from jax import lax

D = 4096
QUERY_HEAD_HALF = 32
KEY_VALUE_HEADS = 4
HEAD_SIZE = 128
FF = 768
TOP = 8
TOK_DEV = 128
PROMPT_COUNT = 8
SPAN_TOKENS = 512
PREFIX_CAPACITY = 256
EXPERTS = 32
CAP = 36
N_SEQ = 4


def draw_queries(key, part):
    offset_start = jnp.clip(jax.random.normal(jax.random.fold_in(key, 21), (PROMPT_COUNT, SPAN_TOKENS, QUERY_HEAD_HALF, HEAD_SIZE), jnp.float32), -6.0, 6.0)
    return offset_start.reshape(PROMPT_COUNT, SPAN_TOKENS, QUERY_HEAD_HALF * HEAD_SIZE).astype(jnp.bfloat16)


def draw_key_cache(key, part):
    offset_start = jnp.clip(jax.random.normal(jax.random.fold_in(key, 31), (PROMPT_COUNT, KEY_VALUE_HEADS, PREFIX_CAPACITY, HEAD_SIZE), jnp.float32), -6.0, 6.0)
    return offset_start.astype(jnp.bfloat16)


def draw_router_weight(key, part):
    offset_start = jnp.clip(jax.random.normal(jax.random.fold_in(key, 41), (D, EXPERTS), jnp.float32), -4.0, 4.0) * D ** (-0.5)
    return offset_start.astype(jnp.bfloat16)


def draw_prefix_len(key, part):
    lengths = jax.random.randint(jax.random.fold_in(key, 51), (PROMPT_COUNT,), 1, PREFIX_CAPACITY + 1)
    chosen = jax.random.randint(jax.random.fold_in(key, 52), (), 0, PROMPT_COUNT)
    return jnp.where(jnp.arange(PROMPT_COUNT) == chosen, PREFIX_CAPACITY, lengths).astype(jnp.int32)


def level_of(key, extent, split, least, high):
    def one(dim, shards_of):
        draws = jax.random.uniform(jax.random.fold_in(jax.random.fold_in(key, 6), dim), (shards_of,), jnp.float32, least / len(split), high / len(split))
        return jnp.repeat(jnp.exp(draws), extent[dim] // shards_of).reshape((-1,) + (1,) * (len(extent) - dim - 1))

    level = one(*split[0])
    for cut in split[1:]:
        level = level * one(*cut)
    return level


def deal_out(key, own, number, rows, number_of, top, bound, lean):
    ranking = jax.random.permutation(key, number_of)
    heavy_load, usual = shares(number_of, rows * top, bound, lean, True), shares(number_of, rows * top, bound, lean, False)
    places = jnp.arange(number_of)

    def named(sizes, offset_by):
        used = int((sizes > 0).sum())
        fixed = max(1, used // 4)
        passed = fixed + (places - fixed + offset_by * (used - fixed)) % max(1, number_of - fixed)
        return jnp.zeros((number_of,), jnp.int32).at[ranking[jnp.where(places < fixed, places, passed)]].set(jnp.asarray(sizes, jnp.int32))

    sizes = jnp.where(number % 4 == 0, named(heavy_load, number // 4), named(usual, number - number // 4 - 1))
    mixed = jax.random.permutation(jax.random.fold_in(own, 3), number_of)
    source_of, taker = mixed[0:number_of // 2 * 2:2], mixed[1:number_of // 2 * 2:2]
    slack = jnp.minimum(sizes[source_of] - 1, bound - sizes[taker]) // 2
    slack = jnp.where((source_of == ranking[0]) | (taker == ranking[0]) | (sizes[taker] == 0), 0, jnp.maximum(slack, 0))
    passed = jax.random.randint(jax.random.fold_in(own, 4), (number_of // 2,), 0, 1 << 20) % (slack + 1)
    sizes = sizes.at[source_of].add(-passed).at[taker].add(passed)
    items = jnp.searchsorted(jnp.cumsum(sizes), jnp.arange(rows * top), side="right").astype(jnp.int32)
    grid = items.reshape(top, rows).T
    grid = grid[jax.random.permutation(jax.random.fold_in(own, 1), rows)]
    offset_by = jax.random.randint(jax.random.fold_in(own, 2), (rows, 1), 0, top)
    return jnp.take_along_axis(grid, (jnp.arange(top)[None, :] + offset_by) % top, axis=1)


def shares(number_of, total, reach, slope, full):
    loads = [(1 << 20) // math.isqrt(grade ** slope) + 1 for grade in range(1, number_of + 1)]
    largest = reach if full else min(reach, max(-(-total // number_of), total * loads[0] // sum(loads)))
    least = 1 if total - largest >= number_of - 1 else 0
    counts, surplus = [largest] + [least] * (number_of - 1), total - largest - least * (number_of - 1)
    while surplus > 0:
        movable = [i for i in range(1, number_of) if counts[i] < largest] or [i for i in range(1, number_of) if counts[i] < reach]
        whole, remaining = sum([loads[i] for i in movable]), surplus
        for i in movable:
            more = min(reach - counts[i], max(1, remaining * loads[i] // whole), surplus)
            counts[i] = counts[i] + more
            surplus = surplus - more
    return np.array(counts)


def normal_values(own_key, dims, scale, limit, shards=(), held_as=jnp.bfloat16):
    loudness = level_of(own_key, dims, shards, -0.22, 0.18) if shards else 1.0
    entries = jax.random.normal(own_key, dims, jnp.float32) * scale * loudness
    return jnp.minimum(jnp.maximum(entries, -limit), limit).astype(held_as)


def setup_inputs(seed: int = 0) -> dict:
    streams_of = jax.random.split(jax.random.key(seed), 15)
    resid = normal_values(streams_of[0], (PROMPT_COUNT, SPAN_TOKENS, D), 0.25, 1.5, ((0, 8), (1, 4)))
    queries = draw_queries(jax.random.fold_in(streams_of[14], 71), 0)
    span_rotated_keys = normal_values(streams_of[2], (PROMPT_COUNT, SPAN_TOKENS, KEY_VALUE_HEADS * HEAD_SIZE), 1.0, 6.0, ((0, 8), (1, 4)))
    span_value_rows = normal_values(streams_of[3], (PROMPT_COUNT, SPAN_TOKENS, KEY_VALUE_HEADS * HEAD_SIZE), 1.0, 6.0, ((0, 8), (1, 4)))
    key_cache = draw_key_cache(jax.random.fold_in(streams_of[14], 71), 0)
    prefix_value_cache = normal_values(streams_of[5], (PROMPT_COUNT, KEY_VALUE_HEADS, PREFIX_CAPACITY, HEAD_SIZE), 1.0, 6.0, ((0, 8), (2, 4)))
    prefix_len = draw_prefix_len(jax.random.fold_in(streams_of[14], 71), 0)
    out_weight = normal_values(streams_of[7], (QUERY_HEAD_HALF * HEAD_SIZE, D), (QUERY_HEAD_HALF * HEAD_SIZE) ** -0.5, 0.09375, ((0, 4),))
    norm_gain = jnp.clip(1.0 + 0.18 * jax.random.normal(streams_of[8], (D,), jnp.float32), 0.1, 1.9)
    router_weight = draw_router_weight(jax.random.fold_in(streams_of[14], 71), 0)
    expert_ids_keys = jax.random.split(jax.random.fold_in(streams_of[10], 1), PROMPT_COUNT * SPAN_TOKENS // TOK_DEV)
    expert_ids_turns = jax.random.permutation(jax.random.fold_in(streams_of[10], 3), PROMPT_COUNT * SPAN_TOKENS // TOK_DEV)
    expert_ids = jax.vmap(lambda own, number: deal_out(jax.random.fold_in(streams_of[10], 2), own, number, TOK_DEV, EXPERTS, TOP, CAP, 2))(expert_ids_keys, expert_ids_turns).reshape((PROMPT_COUNT, SPAN_TOKENS, TOP))
    w_gate = normal_values(streams_of[11], (EXPERTS, D, FF), D ** -0.5, 0.09375, ((0, 32),))
    w_up = normal_values(streams_of[12], (EXPERTS, D, FF), D ** -0.5, 0.09375, ((0, 32),))
    w_down = normal_values(streams_of[13], (EXPERTS, FF, D), FF ** -0.5, 0.21875, ((0, 32),))
    return dict(resid=resid, queries=queries, span_rotated_keys=span_rotated_keys, span_value_rows=span_value_rows, key_cache=key_cache, prefix_value_cache=prefix_value_cache, prefix_len=prefix_len, out_weight=out_weight, norm_gain=norm_gain, router_weight=router_weight, expert_ids=expert_ids, w_gate=w_gate, w_up=w_up, w_down=w_down)


def expert_mlp(token_rows, gate_part, up_part, down_part):
    gate_val = jnp.dot(token_rows, gate_part, preferred_element_type=jnp.float32)
    up_val = jnp.dot(token_rows, up_part, preferred_element_type=jnp.float32)
    activated = (jax.nn.silu(gate_val) * up_val).astype(jnp.bfloat16)
    return jnp.dot(activated, down_part, preferred_element_type=jnp.float32).astype(jnp.bfloat16)

def attend_prompt(inputs):
    query_one, single_prompt_keys, single_prompt_values, cache_keys, cache_values, length = inputs
    group_length = QUERY_HEAD_HALF // KEY_VALUE_HEADS
    span_length = query_one.shape[0]
    prefix_total = cache_keys.shape[1]
    query_block = query_one.reshape(span_length, QUERY_HEAD_HALF, HEAD_SIZE).astype(jnp.float32)
    spanned_key_rows = single_prompt_keys.reshape(span_length, KEY_VALUE_HEADS, HEAD_SIZE).transpose(1, 0, 2)
    spanned_value_rows = single_prompt_values.reshape(span_length, KEY_VALUE_HEADS, HEAD_SIZE).transpose(1, 0, 2)
    all_keys = jnp.repeat(jnp.concatenate([cache_keys, spanned_key_rows], axis=1), group_length, axis=0).astype(jnp.float32)
    all_values = jnp.repeat(jnp.concatenate([cache_values, spanned_value_rows], axis=1), group_length, axis=0).astype(jnp.float32)
    scores = jnp.einsum('thd,hjd->htj', query_block, all_keys) * HEAD_SIZE ** (-0.5)
    position = jnp.arange(prefix_total + span_length, dtype=jnp.int32)
    query_pos = jnp.arange(span_length, dtype=jnp.int32)
    usable_keys = jnp.where(position[None, :] < prefix_total, position[None, :] < length, position[None, :] - prefix_total <= query_pos[:, None])
    scores = jnp.where(usable_keys[None], scores, -1e+30)
    top_score = lax.optimization_barrier(jnp.max(scores, axis=2, keepdims=True))
    raised = jnp.exp(scores - top_score)
    attn_weights = (raised / lax.optimization_barrier(jnp.sum(raised, axis=2, keepdims=True))).astype(jnp.bfloat16)
    attended = jnp.einsum('htj,hjd->thd', attn_weights.astype(jnp.float32), all_values).astype(jnp.bfloat16)
    return attended.reshape(span_length, QUERY_HEAD_HALF * HEAD_SIZE)

def reference(resid, queries, span_rotated_keys, span_value_rows, key_cache, prefix_value_cache, prefix_len, out_weight, norm_gain, router_weight, expert_ids, w_gate, w_up, w_down):
    attended = lax.map(attend_prompt, (queries, span_rotated_keys, span_value_rows, key_cache, prefix_value_cache, prefix_len))
    token_total = PROMPT_COUNT * SPAN_TOKENS
    flat_attn = attended.reshape(token_total, QUERY_HEAD_HALF * HEAD_SIZE)
    group_width = QUERY_HEAD_HALF * HEAD_SIZE // N_SEQ
    projected = jnp.zeros((token_total, D), jnp.float32)
    for group_index in range(N_SEQ):
        lower = group_index * group_width
        partial_sum = jnp.dot(flat_attn[:, lower:lower + group_width], out_weight[lower:lower + group_width], preferred_element_type=jnp.float32).astype(jnp.bfloat16)
        projected = projected + lax.optimization_barrier(partial_sum).astype(jnp.float32)
    hidden_state = resid.reshape(token_total, D).astype(jnp.float32) + projected
    mean_square = lax.optimization_barrier(jnp.mean(hidden_state * hidden_state, axis=1, keepdims=True))
    normed = (hidden_state * lax.rsqrt(mean_square + 1e-06) * norm_gain).astype(jnp.bfloat16)
    logits = jnp.dot(normed, router_weight, preferred_element_type=jnp.float32)
    chosen_ids = expert_ids.reshape(token_total, TOP)
    chosen = jnp.take_along_axis(logits, chosen_ids, axis=1)
    route_weight = jax.nn.softmax(chosen, axis=1)
    block_count = token_total // TOK_DEV
    per_block = TOK_DEV * TOP
    flat_ids = chosen_ids.reshape(block_count, per_block)
    one_hot = (flat_ids[:, :, None] == jnp.arange(EXPERTS, dtype=jnp.int32)[None, None, :]).astype(jnp.int32)
    running_rank = jnp.cumsum(one_hot, axis=1) - 1
    slot_index = lax.optimization_barrier(jnp.sum(one_hot * running_rank, axis=2))
    block_ids = jnp.arange(block_count, dtype=jnp.int32)[:, None]
    buffer_len = block_count * CAP
    target = flat_ids * buffer_len + block_ids * CAP + slot_index
    source_token = block_ids * TOK_DEV + jnp.arange(per_block, dtype=jnp.int32)[None, :] // TOP
    slot_token = jnp.full((EXPERTS * buffer_len,), token_total, jnp.int32).at[target.reshape(-1)].set(source_token.reshape(-1))
    slot_weight = jnp.zeros((EXPERTS * buffer_len,), jnp.float32).at[target.reshape(-1)].set(route_weight.reshape(-1))
    padded = jnp.concatenate([normed, jnp.zeros((1, D), jnp.bfloat16)], axis=0)

    def add_expert(mixture, inputs):
        token_list, weight_list, gate_part, up_part, down_part = inputs
        outputs = expert_mlp(padded[token_list], gate_part, up_part, down_part).astype(jnp.float32)
        return (mixture.at[token_list].add(weight_list[:, None] * outputs, mode='drop'), None)
    mixture, unused = lax.scan(add_expert, jnp.zeros((token_total, D), jnp.float32), (slot_token.reshape(EXPERTS, buffer_len), slot_weight.reshape(EXPERTS, buffer_len), w_gate, w_up, w_down))
    return (hidden_state + mixture).astype(jnp.bfloat16).reshape(PROMPT_COUNT, SPAN_TOKENS, D)
```

```python
import functools

import jax
import jax.numpy as jnp
import numpy as np
from jax import lax
from jax.experimental import pallas as pl
from jax.experimental.pallas import tpu as pltpu
from jax.sharding import PartitionSpec as P

QUERY_HEAD_HALF = 32
KEY_VALUE_HEADS = 4
HEAD_SIZE = 128
TOP = 8


LINE = 4
MESH = pl.DeviceIdType.MESH
VMEM_BYTES = 60 * 1024 * 1024


class Place:
    def __init__(self, line, width, seq_count):
        self.line, self.width, self.plane = line, width, width * seq_count
        self.seq, exp = lax.axis_index("seq"), lax.axis_index("exp")
        self.z, self.x = lax.div(exp, width), lax.rem(exp, width)
        self.me = self.seq * width + self.x

    def on_line(self, k):
        z = lax.rem(self.z + k, self.line)
        return z, {"seq": self.seq, "exp": z * self.width + self.x}

    def in_plane(self, k):
        j = lax.rem(self.me + k, self.plane)
        return j, {
            "seq": lax.div(j, self.width),
            "exp": self.z * self.width + lax.rem(j, self.width),
        }

    def greet(self):
        barrier = pltpu.get_barrier_semaphore()
        for k in range(1, self.line):
            pl.semaphore_signal(
                barrier, inc=1, device_id=self.on_line(k)[1], device_id_type=MESH
            )
        for k in range(1, self.plane):
            pl.semaphore_signal(
                barrier, inc=1, device_id=self.in_plane(k)[1], device_id_type=MESH
            )
        pl.semaphore_wait(barrier, self.line + self.plane - 2)


def span(start, size, step):
    return pl.ds(pl.multiple_of(start * size, step), size)


def remote(src, dst, send, recv, target):
    return pltpu.make_async_remote_copy(
        src_ref=src, dst_ref=dst, send_sem=send, recv_sem=recv,
        device_id=target, device_id_type=MESH,
    )


def dispatch_kernel(
    line, width, seq_count, cap,
    normed_ref, pick_ref, router_ref, gate_hbm, up_hbm,
    act_ref, logit_ref,
    lines, pack, rows_in, gate, up, gate_sum, up_sum,
    line_send, line_recv, plane_send, plane_recv, weight_sem,
):
    at = Place(line, width, seq_count)
    chunks, _, cw = lines.shape
    tokens = normed_ref.shape[0]
    plane = at.plane
    total = plane * cap
    block = total // 4

    def weight_copies(c):
        return (
            pltpu.make_async_copy(gate_hbm.at[span(c, cw, cw)], gate.at[c], weight_sem.at[0, c]),
            pltpu.make_async_copy(up_hbm.at[span(c, cw, cw)], up.at[c], weight_sem.at[1, c]),
        )

    def start_weights(c, carry):
        for copy in weight_copies(c):
            copy.start()
        return carry

    lax.fori_loop(0, chunks, start_weights, 0)
    own = span(at.z, tokens, tokens)
    for c in range(chunks):
        lines[c, own, :] = normed_ref[:, c * cw : (c + 1) * cw]
    gate_sum[...] = jnp.zeros_like(gate_sum)
    up_sum[...] = jnp.zeros_like(up_sum)
    logit_ref[...] = jnp.zeros_like(logit_ref)
    at.greet()

    def line_start(c):
        for k in range(1, line):
            target = at.on_line(k)[1]
            part = lines.at[c, own]
            remote(part, part, line_send.at[c], line_recv.at[c], target).start()

    def line_bulk(c):
        part = lines.at[c, pl.ds(0, (line - 1) * tokens)]
        return remote(part, part, line_send.at[c], line_recv.at[c], at.on_line(1)[1])

    def plane_bulk(c):
        part = pl.ds(0, (plane - 1) * cap)
        return remote(
            pack.at[lax.rem(c, 2), part], rows_in.at[c, part],
            plane_send.at[c], plane_recv.at[c], at.in_plane(1)[1],
        )

    def plane_start(c):
        slot = lax.rem(c, 2)

        @pl.when(c >= 2)
        def _():
            plane_bulk(c - 2).wait_send()

        for b in range(4):
            part = pl.ds(b * block, block)
            pack[slot, part, :] = jnp.dot(
                pick_ref[part, :], lines[c], preferred_element_type=jnp.float32
            ).astype(jnp.bfloat16)
        mine = span(at.me, cap, 16)
        for k in range(1, plane):
            j, target = at.in_plane(k)
            remote(
                pack.at[slot, span(j, cap, 16)], rows_in.at[c, mine],
                plane_send.at[c], plane_recv.at[c], target,
            ).start()
        rows_in[c, mine, :] = pack[slot, mine, :]
        logit_ref[...] += jnp.dot(
            lines[c], router_ref[span(c, cw, cw), :], preferred_element_type=jnp.float32
        )

    def multiply(c):
        for copy in weight_copies(c):
            copy.wait()
        plane_bulk(c).wait_recv()
        for b in range(4):
            part = pl.ds(b * block, block)
            rows = rows_in[c, part, :]
            gate_sum[part, :] += jnp.dot(rows, gate[c], preferred_element_type=jnp.float32)
            up_sum[part, :] += jnp.dot(rows, up[c], preferred_element_type=jnp.float32)

    line_start(0)
    line_start(1)

    def step(c, carry):
        @pl.when(c + 2 < chunks)
        def _():
            line_start(c + 2)

        line_bulk(c).wait_recv()
        plane_start(c)

        @pl.when(c >= 1)
        def _():
            multiply(c - 1)

        return carry

    lax.fori_loop(0, chunks, step, 0)
    multiply(chunks - 1)
    for b in range(4):
        part = pl.ds(b * block, block)
        value = gate_sum[part, :]
        act_ref[part, :] = (value / (1.0 + jnp.exp(-value)) * up_sum[part, :]).astype(jnp.bfloat16)

    def drain(c, carry):
        line_bulk(c).wait_send()
        return carry

    lax.fori_loop(0, chunks, drain, 0)
    plane_bulk(chunks - 2).wait_send()
    plane_bulk(chunks - 1).wait_send()


def return_kernel(
    line, width, seq_count, cap,
    act_ref, mix_ref, hidden_ref, down_hbm,
    out_ref,
    down, made, rows_in, part_out, own_part, parts_in,
    plane_send, plane_recv, line_send, line_recv, weight_sem,
):
    at = Place(line, width, seq_count)
    chunks, _, cw = down.shape
    tokens = hidden_ref.shape[0]
    plane = at.plane
    total = plane * cap
    block = total // 4

    def weight_copy(c):
        return pltpu.make_async_copy(down_hbm.at[:, span(c, cw, cw)], down.at[c], weight_sem.at[c])

    def start_weights(c, carry):
        weight_copy(c).start()
        return carry

    lax.fori_loop(0, chunks, start_weights, 0)
    at.greet()

    def plane_bulk(c):
        part = pl.ds(0, (plane - 1) * cap)
        return remote(
            made.at[lax.rem(c, 2), part], rows_in.at[c, part],
            plane_send.at[c], plane_recv.at[c], at.in_plane(1)[1],
        )

    def line_bulk(c):
        return remote(
            part_out.at[lax.rem(c, 2)], parts_in.at[c],
            line_send.at[c], line_recv.at[c], at.on_line(1)[1],
        )

    def down_step(c):
        slot = lax.rem(c, 2)
        weight_copy(c).wait()

        @pl.when(c >= 2)
        def _():
            plane_bulk(c - 2).wait_send()

        for b in range(4):
            part = pl.ds(b * block, block)
            made[slot, part, :] = jnp.dot(
                act_ref[part, :], down[c], preferred_element_type=jnp.float32
            ).astype(jnp.bfloat16)
        mine = span(at.me, cap, 16)
        for k in range(1, plane):
            j, target = at.in_plane(k)
            remote(
                made.at[slot, span(j, cap, 16)], rows_in.at[c, mine],
                plane_send.at[c], plane_recv.at[c], target,
            ).start()
        rows_in[c, mine, :] = made[slot, mine, :]

    def merge_step(c):
        slot = lax.rem(c, 2)
        plane_bulk(c).wait_recv()

        @pl.when(c >= 2)
        def _():
            line_bulk(c - 2).wait_send()

        for k in range(1, line + 1):
            z, target = at.on_line(k)
            part = jnp.dot(
                mix_ref[span(z, tokens, tokens), :], rows_in[c],
                preferred_element_type=jnp.float32,
            )
            if k == line:
                own_part[slot] = part
            else:
                part_out[slot, k - 1] = part.astype(jnp.bfloat16)
                remote(
                    part_out.at[slot, k - 1], parts_in.at[c, k - 1],
                    line_send.at[c], line_recv.at[c], target,
                ).start()

    def finish_step(c):
        line_bulk(c).wait_recv()
        columns = span(c, cw, cw)
        value = hidden_ref[:, columns] + own_part[lax.rem(c, 2)]
        for k in range(line - 1):
            value += parts_in[c, k].astype(jnp.float32)
        out_ref[:, columns] = value.astype(jnp.bfloat16)

    def step(c, carry):
        @pl.when(c < chunks)
        def _():
            down_step(c)

        @pl.when((c >= 1) & (c <= chunks))
        def _():
            merge_step(c - 1)

        @pl.when(c >= 2)
        def _():
            finish_step(c - 2)

        return carry

    lax.fori_loop(0, chunks + 2, step, 0)
    for c in (chunks - 2, chunks - 1):
        plane_bulk(c).wait_send()
        line_bulk(c).wait_send()


def kernel_params(collective_id):
    return pltpu.CompilerParams(
        collective_id=collective_id, has_side_effects=True, vmem_limit_bytes=VMEM_BYTES
    )


def experts_layer(hidden_state, normed, router_weight, chosen_ids, w_gate, w_up, w_down):
    seq_count, exp_count = lax.axis_size("seq"), lax.axis_size("exp")
    tokens, width_d = normed.shape
    line, width = LINE, exp_count // LINE
    plane = seq_count * width
    experts = seq_count * exp_count
    hidden_units = w_gate.shape[1]
    per_block = max(2, (tokens * TOP * 9 + 8 * experts - 1) // (8 * experts))
    cap = (line * per_block + 15) // 16 * 16
    total = plane * cap
    group = line * tokens
    chunks = 8
    cw = width_d // chunks
    bf16, f32 = jnp.bfloat16, jnp.float32

    rings = [[z * width + x for z in range(line)] for x in range(width)]
    ids = lax.all_gather(chosen_ids, "exp", axis_index_groups=rings, tiled=True)
    named = jnp.any(ids[:, :, None] == jnp.arange(experts, dtype=jnp.int32), axis=1)
    my_z = lax.axis_index("exp") // width
    here = lax.dynamic_slice_in_dim(
        named.reshape(group, seq_count, line, width), my_z, 1, axis=2
    ).reshape(group, plane)
    before = jnp.asarray(np.tril(np.ones((group, group)), -1), bf16)
    rank = jnp.dot(before, here.astype(bf16), preferred_element_type=f32)
    place = jnp.where(here, rank, -1.0).astype(jnp.int32)
    seats = jnp.arange(cap, dtype=jnp.int32)
    pick = (place.T[:, None, :] == seats[None, :, None]).astype(bf16).reshape(total, group)

    vmem = pl.BlockSpec(memory_space=pltpu.VMEM)
    hbm = pl.BlockSpec(memory_space=pl.ANY)
    dma = pltpu.SemaphoreType.DMA
    act, logits = pl.pallas_call(
        functools.partial(dispatch_kernel, line, width, seq_count, cap),
        out_shape=(
            jax.ShapeDtypeStruct((total, hidden_units), bf16),
            jax.ShapeDtypeStruct((group, experts), f32),
        ),
        in_specs=[vmem, vmem, vmem, hbm, hbm],
        out_specs=(vmem, vmem),
        scratch_shapes=[
            pltpu.VMEM((chunks, group, cw), bf16),
            pltpu.VMEM((2, total, cw), bf16),
            pltpu.VMEM((chunks, total, cw), bf16),
            pltpu.VMEM((chunks, cw, hidden_units), bf16),
            pltpu.VMEM((chunks, cw, hidden_units), bf16),
            pltpu.VMEM((total, hidden_units), f32),
            pltpu.VMEM((total, hidden_units), f32),
            dma((chunks,)), dma((chunks,)), dma((chunks,)), dma((chunks,)), dma((2, chunks)),
        ],
        compiler_params=kernel_params(0),
        name="dispatch",
    )(normed, pick, router_weight, w_gate, w_up)

    masked = jnp.where(named, logits, -jnp.inf)
    raised = jnp.exp(masked - jnp.max(masked, axis=1, keepdims=True))
    route_weight = raised / jnp.sum(raised, axis=1, keepdims=True)
    weight_here = lax.dynamic_slice_in_dim(
        route_weight.reshape(group, seq_count, line, width), my_z, 1, axis=2
    ).reshape(group, plane)
    mix = jnp.where(place[:, :, None] == seats, weight_here[:, :, None], 0.0)
    mix = mix.astype(bf16).reshape(group, total)

    return pl.pallas_call(
        functools.partial(return_kernel, line, width, seq_count, cap),
        out_shape=jax.ShapeDtypeStruct((tokens, width_d), bf16),
        in_specs=[vmem, vmem, vmem, hbm],
        out_specs=vmem,
        scratch_shapes=[
            pltpu.VMEM((chunks, hidden_units, cw), bf16),
            pltpu.VMEM((2, total, cw), bf16),
            pltpu.VMEM((chunks, total, cw), bf16),
            pltpu.VMEM((2, line - 1, tokens, cw), bf16),
            pltpu.VMEM((2, tokens, cw), f32),
            pltpu.VMEM((chunks, line - 1, tokens, cw), bf16),
            dma((chunks,)), dma((chunks,)), dma((chunks,)), dma((chunks,)), dma((chunks,)),
        ],
        compiler_params=kernel_params(1),
        name="give_back",
    )(act, mix, hidden_state, w_down)


def per_device(
    resid,
    queries,
    span_rotated_keys,
    span_value_rows,
    key_cache,
    prefix_value_cache,
    prefix_len,
    out_weight,
    norm_gain,
    router_weight,
    expert_ids,
    w_gate,
    w_up,
    w_down,
):
    seq_count = lax.axis_size("seq")
    exp_count = lax.axis_size("exp")
    token_row_block = queries.shape[1]
    model_width = resid.shape[2]
    heads_here = QUERY_HEAD_HALF // seq_count
    group_length = QUERY_HEAD_HALF // KEY_VALUE_HEADS
    key_value_choice = np.arange(seq_count) * heads_here // group_length
    query_parts = queries[0].reshape(token_row_block, seq_count, heads_here * HEAD_SIZE)
    newest_keys = span_rotated_keys[0].reshape(token_row_block, KEY_VALUE_HEADS, HEAD_SIZE)[
        :, key_value_choice, :
    ]
    newest_values = span_value_rows[0].reshape(token_row_block, KEY_VALUE_HEADS, HEAD_SIZE)[
        :, key_value_choice, :
    ]
    fresh_pairs = jnp.concatenate([newest_keys, newest_values], axis=2)
    query_heads, span_pairs = (
        lax.all_to_all(query_parts, "seq", split_axis=1, concat_axis=0, tiled=True),
        lax.all_to_all(fresh_pairs, "seq", split_axis=1, concat_axis=0, tiled=True),
    )
    cache_pairs = jnp.concatenate(
        [key_cache[0][key_value_choice], prefix_value_cache[0][key_value_choice]], axis=2
    )
    prefix_pairs = lax.all_to_all(cache_pairs, "seq", split_axis=0, concat_axis=1, tiled=True)[0]
    span_length = query_heads.shape[0]
    prefix_total = prefix_pairs.shape[0]
    all_keys = jnp.concatenate([prefix_pairs[:, :HEAD_SIZE], span_pairs[:, 0, :HEAD_SIZE]], axis=0)
    all_values = jnp.concatenate(
        [prefix_pairs[:, HEAD_SIZE:], span_pairs[:, 0, HEAD_SIZE:]], axis=0
    )
    query_block = query_heads.reshape(span_length, heads_here, HEAD_SIZE)
    scores = jnp.einsum(
        "thd,jd->htj", query_block, all_keys, preferred_element_type=jnp.float32
    ) * HEAD_SIZE ** (-0.5)
    position = jnp.arange(prefix_total + span_length, dtype=jnp.int32)
    query_pos = jnp.arange(span_length, dtype=jnp.int32)
    usable_keys = jnp.where(
        position[None, :] < prefix_total,
        position[None, :] < prefix_len[0],
        position[None, :] - prefix_total <= query_pos[:, None],
    )
    scores = jnp.where(usable_keys[None], scores, -1e30)
    top_score = jnp.max(scores, axis=2, keepdims=True)
    raised = jnp.exp(scores - top_score)
    attn_weights = (raised / jnp.sum(raised, axis=2, keepdims=True)).astype(jnp.bfloat16)
    attended = jnp.einsum(
        "htj,jd->thd", attn_weights, all_values, preferred_element_type=jnp.float32
    ).astype(jnp.bfloat16)
    attended = attended.reshape(span_length, heads_here * HEAD_SIZE)
    projected = lax.psum_scatter(
        jnp.dot(attended, out_weight, preferred_element_type=jnp.float32).astype(jnp.bfloat16),
        "seq",
        scatter_dimension=0,
        tiled=True,
    ).astype(jnp.float32)
    hidden_state = resid[0].astype(jnp.float32) + projected
    mean_square = jnp.mean(hidden_state * hidden_state, axis=1, keepdims=True)
    normed = (hidden_state * lax.rsqrt(mean_square + 1e-06) * norm_gain).astype(jnp.bfloat16)
    out = experts_layer(
        hidden_state, normed, router_weight, expert_ids[0], w_gate[0], w_up[0], w_down[0]
    )
    return out[None]


def solution(mesh):
    in_specs = (
        P("exp", "seq", None),
        P("exp", "seq", None),
        P("exp", "seq", None),
        P("exp", "seq", None),
        P("exp", None, "seq", None),
        P("exp", None, "seq", None),
        P("exp"),
        P("seq", None),
        P(),
        P(),
        P("exp", "seq", None),
        P(("seq", "exp"), None, None),
        P(("seq", "exp"), None, None),
        P(("seq", "exp"), None, None),
    )
    out_specs = P("exp", "seq", None)
    return jax.shard_map(
        per_device, mesh=mesh, in_specs=in_specs, out_specs=out_specs, check_vma=False
    )
```

```python
import functools

import jax
import jax.numpy as jnp
import numpy as np
from jax import lax
from jax.experimental import pallas as pl
from jax.experimental.pallas import tpu as pltpu
from jax.sharding import PartitionSpec as P

QUERY_HEAD_HALF = 32
KEY_VALUE_HEADS = 4
HEAD_SIZE = 128
TOP = 8


LINE = 4
MESH = pl.DeviceIdType.MESH
VMEM_BYTES = 60 * 1024 * 1024


class Place:
    def __init__(self, line, width, seq_count):
        self.line, self.width, self.plane = line, width, width * seq_count
        self.seq, exp = lax.axis_index("seq"), lax.axis_index("exp")
        self.z, self.x = lax.div(exp, width), lax.rem(exp, width)
        self.me = self.seq * width + self.x

    def on_line(self, k):
        z = lax.rem(self.z + k, self.line)
        return z, {"seq": self.seq, "exp": z * self.width + self.x}

    def in_plane(self, k):
        j = lax.rem(self.me + k, self.plane)
        return j, {
            "seq": lax.div(j, self.width),
            "exp": self.z * self.width + lax.rem(j, self.width),
        }

    def greet(self):
        barrier = pltpu.get_barrier_semaphore()
        for k in range(1, self.line):
            pl.semaphore_signal(
                barrier, inc=1, device_id=self.on_line(k)[1], device_id_type=MESH
            )
        for k in range(1, self.plane):
            pl.semaphore_signal(
                barrier, inc=1, device_id=self.in_plane(k)[1], device_id_type=MESH
            )
        pl.semaphore_wait(barrier, self.line + self.plane - 2)


def span(start, size, step):
    return pl.ds(pl.multiple_of(start * size, step), size)


def remote(src, dst, send, recv, target):
    return pltpu.make_async_remote_copy(
        src_ref=src, dst_ref=dst, send_sem=send, recv_sem=recv,
        device_id=target, device_id_type=MESH,
    )


def dispatch_kernel(
    line, width, seq_count, cap,
    normed_ref, ids_ref, homes_ref, router_ref, gate_hbm, up_hbm,
    act_ref, mix_ref,
    ids, pick, mix_turned, logits, lines, pack, rows_in, gate, up, gate_sum, up_sum,
    line_send, line_recv, plane_send, plane_recv, weight_sem, ids_send, ids_recv,
):
    at = Place(line, width, seq_count)
    chunks, _, cw = lines.shape
    tokens = normed_ref.shape[0]
    plane = at.plane
    total = plane * cap
    block = total // 4

    def weight_copies(c):
        return (
            pltpu.make_async_copy(gate_hbm.at[span(c, cw, cw)], gate.at[c], weight_sem.at[0, c]),
            pltpu.make_async_copy(up_hbm.at[span(c, cw, cw)], up.at[c], weight_sem.at[1, c]),
        )

    def start_weights(c, carry):
        for copy in weight_copies(c):
            copy.start()
        return carry

    lax.fori_loop(0, chunks, start_weights, 0)
    own = span(at.z, tokens, tokens)
    ids[own, :] = ids_ref[...]
    for c in range(chunks):
        lines[c, own, :] = normed_ref[:, c * cw : (c + 1) * cw]
    gate_sum[...] = jnp.zeros_like(gate_sum)
    up_sum[...] = jnp.zeros_like(up_sum)
    logits[...] = jnp.zeros_like(logits)
    at.greet()
    for k in range(1, line):
        remote(ids.at[own], ids.at[own], ids_send, ids_recv, at.on_line(k)[1]).start()

    def line_start(c):
        for k in range(1, line):
            target = at.on_line(k)[1]
            part = lines.at[c, own]
            remote(part, part, line_send.at[c], line_recv.at[c], target).start()

    def line_bulk(c):
        part = lines.at[c, pl.ds(0, (line - 1) * tokens)]
        return remote(part, part, line_send.at[c], line_recv.at[c], at.on_line(1)[1])

    def plane_bulk(c):
        part = pl.ds(0, (plane - 1) * cap)
        return remote(
            pack.at[lax.rem(c, 2), part], rows_in.at[c, part],
            plane_send.at[c], plane_recv.at[c], at.in_plane(1)[1],
        )

    def plane_start(c):
        slot = lax.rem(c, 2)

        @pl.when(c >= 2)
        def _():
            plane_bulk(c - 2).wait_send()

        for b in range(4):
            part = pl.ds(b * block, block)
            pack[slot, part, :] = jnp.dot(
                pick[part, :], lines[c], preferred_element_type=jnp.float32
            ).astype(jnp.bfloat16)
        mine = span(at.me, cap, 16)
        for k in range(1, plane):
            j, target = at.in_plane(k)
            remote(
                pack.at[slot, span(j, cap, 16)], rows_in.at[c, mine],
                plane_send.at[c], plane_recv.at[c], target,
            ).start()
        rows_in[c, mine, :] = pack[slot, mine, :]
        logits[...] += jnp.dot(
            lines[c], router_ref[span(c, cw, cw), :], preferred_element_type=jnp.float32
        )

    def multiply(c):
        for copy in weight_copies(c):
            copy.wait()
        plane_bulk(c).wait_recv()
        for b in range(4):
            part = pl.ds(b * block, block)
            rows = rows_in[c, part, :]
            gate_sum[part, :] += jnp.dot(rows, gate[c], preferred_element_type=jnp.float32)
            up_sum[part, :] += jnp.dot(rows, up[c], preferred_element_type=jnp.float32)

    def named(experts):
        hits = jnp.zeros((ids.shape[0], experts.shape[1]), jnp.float32)
        for k in range(TOP):
            hits += jnp.where(ids[:, k : k + 1] == experts, 1.0, 0.0)
        return hits

    def iota(shape, axis):
        return lax.broadcasted_iota(jnp.int32, shape, axis)

    line_start(0)
    line_start(1)
    group = ids.shape[0]
    ids_part = ids.at[pl.ds(0, (line - 1) * tokens)]
    ids_bulk = remote(ids_part, ids_part, ids_send, ids_recv, at.on_line(1)[1])
    ids_bulk.wait_recv()
    experts_here = homes_ref[...] + at.z * width
    hits = named(experts_here)
    before = jnp.where(iota((group, group), 1) < iota((group, group), 0), 1.0, 0.0)
    rank = jnp.dot(
        before.astype(jnp.bfloat16), hits.astype(jnp.bfloat16), preferred_element_type=jnp.float32
    )
    place = jnp.where(hits > 0.0, rank, -1.0).T
    seats = iota((cap, group), 0).astype(jnp.float32)
    for j in range(plane):
        seated = jnp.where(place[j : j + 1, :] == seats, 1.0, 0.0)
        pick[j * cap : (j + 1) * cap, :] = seated.astype(jnp.bfloat16)

    def step(c, carry):
        @pl.when(c + 2 < chunks)
        def _():
            line_start(c + 2)

        line_bulk(c).wait_recv()
        plane_start(c)

        @pl.when(c >= 1)
        def _():
            multiply(c - 1)

        return carry

    lax.fori_loop(0, chunks, step, 0)
    experts = logits.shape[1]
    masked = jnp.where(named(iota((1, experts), 1)) > 0.0, logits[...], -jnp.inf)
    raised = jnp.exp(masked - jnp.max(masked, axis=1, keepdims=True))
    weights = raised / jnp.sum(raised, axis=1, keepdims=True)
    select = jnp.where(iota((experts, experts_here.shape[1]), 0) == experts_here, 1.0, 0.0)
    weights_here = jnp.dot(
        weights.astype(jnp.bfloat16), select.astype(jnp.bfloat16),
        preferred_element_type=jnp.float32,
    ).T
    for j in range(plane):
        seat = pick[j * cap : (j + 1) * cap, :].astype(jnp.float32)
        mix_turned[j * cap : (j + 1) * cap, :] = weights_here[j : j + 1, :] * seat
    for b in range(total // 128):
        part = slice(b * 128, (b + 1) * 128)
        mix_ref[:, part] = mix_turned[part, :].T.astype(jnp.bfloat16)
    multiply(chunks - 1)
    for b in range(4):
        part = pl.ds(b * block, block)
        value = gate_sum[part, :]
        act_ref[part, :] = (value / (1.0 + jnp.exp(-value)) * up_sum[part, :]).astype(jnp.bfloat16)

    def drain(c, carry):
        line_bulk(c).wait_send()
        return carry

    lax.fori_loop(0, chunks, drain, 0)
    ids_bulk.wait_send()
    plane_bulk(chunks - 2).wait_send()
    plane_bulk(chunks - 1).wait_send()


def return_kernel(
    line, width, seq_count, cap,
    act_ref, mix_ref, hidden_ref, down_hbm,
    out_ref,
    down, made, rows_in, part_out, own_part, parts_in,
    plane_send, plane_recv, line_send, line_recv, weight_sem,
):
    at = Place(line, width, seq_count)
    chunks, _, cw = down.shape
    tokens = hidden_ref.shape[0]
    plane = at.plane
    total = plane * cap
    block = total // 4

    def weight_copy(c):
        return pltpu.make_async_copy(down_hbm.at[:, span(c, cw, cw)], down.at[c], weight_sem.at[c])

    def start_weights(c, carry):
        weight_copy(c).start()
        return carry

    lax.fori_loop(0, chunks, start_weights, 0)
    at.greet()

    def plane_bulk(c):
        part = pl.ds(0, (plane - 1) * cap)
        return remote(
            made.at[lax.rem(c, 2), part], rows_in.at[c, part],
            plane_send.at[c], plane_recv.at[c], at.in_plane(1)[1],
        )

    def line_bulk(c):
        return remote(
            part_out.at[lax.rem(c, 2)], parts_in.at[c],
            line_send.at[c], line_recv.at[c], at.on_line(1)[1],
        )

    def down_step(c):
        slot = lax.rem(c, 2)
        weight_copy(c).wait()

        @pl.when(c >= 2)
        def _():
            plane_bulk(c - 2).wait_send()

        for b in range(4):
            part = pl.ds(b * block, block)
            made[slot, part, :] = jnp.dot(
                act_ref[part, :], down[c], preferred_element_type=jnp.float32
            ).astype(jnp.bfloat16)
        mine = span(at.me, cap, 16)
        for k in range(1, plane):
            j, target = at.in_plane(k)
            remote(
                made.at[slot, span(j, cap, 16)], rows_in.at[c, mine],
                plane_send.at[c], plane_recv.at[c], target,
            ).start()
        rows_in[c, mine, :] = made[slot, mine, :]

    def merge_step(c):
        slot = lax.rem(c, 2)
        plane_bulk(c).wait_recv()

        @pl.when(c >= 2)
        def _():
            line_bulk(c - 2).wait_send()

        for k in range(1, line + 1):
            z, target = at.on_line(k)
            part = jnp.dot(
                mix_ref[span(z, tokens, tokens), :], rows_in[c],
                preferred_element_type=jnp.float32,
            )
            if k == line:
                own_part[slot] = part
            else:
                part_out[slot, k - 1] = part.astype(jnp.bfloat16)
                remote(
                    part_out.at[slot, k - 1], parts_in.at[c, k - 1],
                    line_send.at[c], line_recv.at[c], target,
                ).start()

    def finish_step(c):
        line_bulk(c).wait_recv()
        columns = span(c, cw, cw)
        value = hidden_ref[:, columns] + own_part[lax.rem(c, 2)]
        for k in range(line - 1):
            value += parts_in[c, k].astype(jnp.float32)
        out_ref[:, columns] = value.astype(jnp.bfloat16)

    def step(c, carry):
        @pl.when(c < chunks)
        def _():
            down_step(c)

        @pl.when((c >= 1) & (c <= chunks))
        def _():
            merge_step(c - 1)

        @pl.when(c >= 2)
        def _():
            finish_step(c - 2)

        return carry

    lax.fori_loop(0, chunks + 2, step, 0)
    for c in (chunks - 2, chunks - 1):
        plane_bulk(c).wait_send()
        line_bulk(c).wait_send()


def kernel_params(collective_id):
    return pltpu.CompilerParams(
        collective_id=collective_id, has_side_effects=True, vmem_limit_bytes=VMEM_BYTES
    )


def experts_layer(hidden_state, normed, router_weight, chosen_ids, w_gate, w_up, w_down):
    seq_count, exp_count = lax.axis_size("seq"), lax.axis_size("exp")
    tokens, width_d = normed.shape
    line, width = LINE, exp_count // LINE
    plane = seq_count * width
    experts = seq_count * exp_count
    hidden_units = w_gate.shape[1]
    per_block = max(2, (tokens * TOP * 9 + 8 * experts - 1) // (8 * experts))
    cap = (line * per_block + 15) // 16 * 16
    total = plane * cap
    group = line * tokens
    chunks = 16
    cw = width_d // chunks
    bf16, f32 = jnp.bfloat16, jnp.float32

    homes = np.full((1, 128), -experts, np.int32)
    homes[0, :plane] = [j // width * exp_count + j % width for j in range(plane)]

    vmem = pl.BlockSpec(memory_space=pltpu.VMEM)
    hbm = pl.BlockSpec(memory_space=pl.ANY)
    dma = pltpu.SemaphoreType.DMA
    act, mix = pl.pallas_call(
        functools.partial(dispatch_kernel, line, width, seq_count, cap),
        out_shape=(
            jax.ShapeDtypeStruct((total, hidden_units), bf16),
            jax.ShapeDtypeStruct((group, total), bf16),
        ),
        in_specs=[vmem, vmem, vmem, vmem, hbm, hbm],
        out_specs=(vmem, vmem),
        scratch_shapes=[
            pltpu.VMEM((group, TOP), jnp.int32),
            pltpu.VMEM((total, group), bf16),
            pltpu.VMEM((total, group), f32),
            pltpu.VMEM((group, experts), f32),
            pltpu.VMEM((chunks, group, cw), bf16),
            pltpu.VMEM((2, total, cw), bf16),
            pltpu.VMEM((chunks, total, cw), bf16),
            pltpu.VMEM((chunks, cw, hidden_units), bf16),
            pltpu.VMEM((chunks, cw, hidden_units), bf16),
            pltpu.VMEM((total, hidden_units), f32),
            pltpu.VMEM((total, hidden_units), f32),
            dma((chunks,)), dma((chunks,)), dma((chunks,)), dma((chunks,)), dma((2, chunks)),
            dma, dma,
        ],
        compiler_params=kernel_params(0),
        name="dispatch",
    )(normed, chosen_ids, jnp.asarray(homes), router_weight, w_gate, w_up)

    return pl.pallas_call(
        functools.partial(return_kernel, line, width, seq_count, cap),
        out_shape=jax.ShapeDtypeStruct((tokens, width_d), bf16),
        in_specs=[vmem, vmem, vmem, hbm],
        out_specs=vmem,
        scratch_shapes=[
            pltpu.VMEM((chunks, hidden_units, cw), bf16),
            pltpu.VMEM((2, total, cw), bf16),
            pltpu.VMEM((chunks, total, cw), bf16),
            pltpu.VMEM((2, line - 1, tokens, cw), bf16),
            pltpu.VMEM((2, tokens, cw), f32),
            pltpu.VMEM((chunks, line - 1, tokens, cw), bf16),
            dma((chunks,)), dma((chunks,)), dma((chunks,)), dma((chunks,)), dma((chunks,)),
        ],
        compiler_params=kernel_params(1),
        name="give_back",
    )(act, mix, hidden_state, w_down)


def per_device(
    resid,
    queries,
    span_rotated_keys,
    span_value_rows,
    key_cache,
    prefix_value_cache,
    prefix_len,
    out_weight,
    norm_gain,
    router_weight,
    expert_ids,
    w_gate,
    w_up,
    w_down,
):
    seq_count = lax.axis_size("seq")
    exp_count = lax.axis_size("exp")
    token_row_block = queries.shape[1]
    model_width = resid.shape[2]
    heads_here = QUERY_HEAD_HALF // seq_count
    group_length = QUERY_HEAD_HALF // KEY_VALUE_HEADS
    key_value_choice = np.arange(seq_count) * heads_here // group_length
    query_parts = queries[0].reshape(token_row_block, seq_count, heads_here * HEAD_SIZE)
    newest_keys = span_rotated_keys[0].reshape(token_row_block, KEY_VALUE_HEADS, HEAD_SIZE)[
        :, key_value_choice, :
    ]
    newest_values = span_value_rows[0].reshape(token_row_block, KEY_VALUE_HEADS, HEAD_SIZE)[
        :, key_value_choice, :
    ]
    fresh_pairs = jnp.concatenate([newest_keys, newest_values], axis=2)
    query_heads, span_pairs = (
        lax.all_to_all(query_parts, "seq", split_axis=1, concat_axis=0, tiled=True),
        lax.all_to_all(fresh_pairs, "seq", split_axis=1, concat_axis=0, tiled=True),
    )
    cache_pairs = jnp.concatenate(
        [key_cache[0][key_value_choice], prefix_value_cache[0][key_value_choice]], axis=2
    )
    prefix_pairs = lax.all_to_all(cache_pairs, "seq", split_axis=0, concat_axis=1, tiled=True)[0]
    span_length = query_heads.shape[0]
    prefix_total = prefix_pairs.shape[0]
    all_keys = jnp.concatenate([prefix_pairs[:, :HEAD_SIZE], span_pairs[:, 0, :HEAD_SIZE]], axis=0)
    all_values = jnp.concatenate(
        [prefix_pairs[:, HEAD_SIZE:], span_pairs[:, 0, HEAD_SIZE:]], axis=0
    )
    query_block = query_heads.reshape(span_length, heads_here, HEAD_SIZE)
    scores = jnp.einsum(
        "thd,jd->htj", query_block, all_keys, preferred_element_type=jnp.float32
    ) * HEAD_SIZE ** (-0.5)
    position = jnp.arange(prefix_total + span_length, dtype=jnp.int32)
    query_pos = jnp.arange(span_length, dtype=jnp.int32)
    usable_keys = jnp.where(
        position[None, :] < prefix_total,
        position[None, :] < prefix_len[0],
        position[None, :] - prefix_total <= query_pos[:, None],
    )
    scores = jnp.where(usable_keys[None], scores, -1e30)
    top_score = jnp.max(scores, axis=2, keepdims=True)
    raised = jnp.exp(scores - top_score)
    attn_weights = (raised / jnp.sum(raised, axis=2, keepdims=True)).astype(jnp.bfloat16)
    attended = jnp.einsum(
        "htj,jd->thd", attn_weights, all_values, preferred_element_type=jnp.float32
    ).astype(jnp.bfloat16)
    attended = attended.reshape(span_length, heads_here * HEAD_SIZE)
    projected = lax.psum_scatter(
        jnp.dot(attended, out_weight, preferred_element_type=jnp.float32).astype(jnp.bfloat16),
        "seq",
        scatter_dimension=0,
        tiled=True,
    ).astype(jnp.float32)
    hidden_state = resid[0].astype(jnp.float32) + projected
    mean_square = jnp.mean(hidden_state * hidden_state, axis=1, keepdims=True)
    normed = (hidden_state * lax.rsqrt(mean_square + 1e-06) * norm_gain).astype(jnp.bfloat16)
    out = experts_layer(
        hidden_state, normed, router_weight, expert_ids[0], w_gate[0], w_up[0], w_down[0]
    )
    return out[None]


def solution(mesh):
    in_specs = (
        P("exp", "seq", None),
        P("exp", "seq", None),
        P("exp", "seq", None),
        P("exp", "seq", None),
        P("exp", None, "seq", None),
        P("exp", None, "seq", None),
        P("exp"),
        P("seq", None),
        P(),
        P(),
        P("exp", "seq", None),
        P(("seq", "exp"), None, None),
        P(("seq", "exp"), None, None),
        P(("seq", "exp"), None, None),
    )
    out_specs = P("exp", "seq", None)
    return jax.shard_map(
        per_device, mesh=mesh, in_specs=in_specs, out_specs=out_specs, check_vma=False
    )
```

```python
import functools

import jax
import jax.numpy as jnp
import numpy as np
from jax import lax
from jax.experimental import pallas as pl
from jax.experimental.pallas import tpu as pltpu
from jax.sharding import PartitionSpec as P

QUERY_HEAD_HALF = 32
KEY_VALUE_HEADS = 4
HEAD_SIZE = 128
TOP = 8


LINE = 4
MESH = pl.DeviceIdType.MESH
VMEM_BYTES = 60 * 1024 * 1024


class Place:
    def __init__(self, line, width, seq_count):
        self.line, self.width, self.plane = line, width, width * seq_count
        self.seq, exp = lax.axis_index("seq"), lax.axis_index("exp")
        self.z, self.x = lax.div(exp, width), lax.rem(exp, width)
        self.me = self.seq * width + self.x

    def on_line(self, k):
        z = lax.rem(self.z + k, self.line)
        return z, {"seq": self.seq, "exp": z * self.width + self.x}

    def in_plane(self, k):
        j = lax.rem(self.me + k, self.plane)
        return j, {
            "seq": lax.div(j, self.width),
            "exp": self.z * self.width + lax.rem(j, self.width),
        }

    def greet(self):
        barrier = pltpu.get_barrier_semaphore()
        for k in range(1, self.line):
            pl.semaphore_signal(
                barrier, inc=1, device_id=self.on_line(k)[1], device_id_type=MESH
            )
        for k in range(1, self.plane):
            pl.semaphore_signal(
                barrier, inc=1, device_id=self.in_plane(k)[1], device_id_type=MESH
            )
        pl.semaphore_wait(barrier, self.line + self.plane - 2)


def span(start, size, step):
    return pl.ds(pl.multiple_of(start * size, step), size)


def remote(src, dst, send, recv, target):
    return pltpu.make_async_remote_copy(
        src_ref=src, dst_ref=dst, send_sem=send, recv_sem=recv,
        device_id=target, device_id_type=MESH,
    )


def dispatch_kernel(
    line, width, seq_count, cap,
    normed_ref, ids_ref, homes_ref, router_ref, gate_hbm, up_hbm,
    act_ref, mix_ref,
    ids, pick, mix_turned, logits, lines, pack, rows_in, gate, up, gate_sum, up_sum,
    line_send, line_recv, plane_send, plane_recv, weight_sem, ids_send, ids_recv,
):
    at = Place(line, width, seq_count)
    chunks, _, cw = lines.shape
    tokens = normed_ref.shape[0]
    plane = at.plane
    total = plane * cap
    block = total // 4

    def weight_copies(c):
        return (
            pltpu.make_async_copy(gate_hbm.at[span(c, cw, cw)], gate.at[c], weight_sem.at[0, c]),
            pltpu.make_async_copy(up_hbm.at[span(c, cw, cw)], up.at[c], weight_sem.at[1, c]),
        )

    def start_weights(c, carry):
        for copy in weight_copies(c):
            copy.start()
        return carry

    lax.fori_loop(0, chunks, start_weights, 0)
    own = span(at.z, tokens, tokens)
    ids[own, :] = ids_ref[...]
    for c in range(chunks):
        lines[c, own, :] = normed_ref[:, c * cw : (c + 1) * cw]
    gate_sum[...] = jnp.zeros_like(gate_sum)
    up_sum[...] = jnp.zeros_like(up_sum)
    logits[...] = jnp.zeros_like(logits)
    at.greet()
    for k in range(1, line):
        remote(ids.at[own], ids.at[own], ids_send, ids_recv, at.on_line(k)[1]).start()

    def line_start(c):
        for k in range(1, line):
            target = at.on_line(k)[1]
            part = lines.at[c, own]
            remote(part, part, line_send.at[c], line_recv.at[c], target).start()

    def line_bulk(c):
        part = lines.at[c, pl.ds(0, (line - 1) * tokens)]
        return remote(part, part, line_send.at[c], line_recv.at[c], at.on_line(1)[1])

    def plane_bulk(c):
        part = pl.ds(0, (plane - 1) * cap)
        return remote(
            pack.at[lax.rem(c, 2), part], rows_in.at[c, part],
            plane_send.at[c], plane_recv.at[c], at.in_plane(1)[1],
        )

    def plane_start(c):
        slot = lax.rem(c, 2)

        @pl.when(c >= 2)
        def _():
            plane_bulk(c - 2).wait_send()

        for b in range(4):
            part = pl.ds(b * block, block)
            pack[slot, part, :] = jnp.dot(
                pick[part, :], lines[c], preferred_element_type=jnp.float32
            ).astype(jnp.bfloat16)
        mine = span(at.me, cap, 16)
        for k in range(1, plane):
            j, target = at.in_plane(k)
            remote(
                pack.at[slot, span(j, cap, 16)], rows_in.at[c, mine],
                plane_send.at[c], plane_recv.at[c], target,
            ).start()
        rows_in[c, mine, :] = pack[slot, mine, :]
        logits[...] += jnp.dot(
            lines[c], router_ref[span(c, cw, cw), :], preferred_element_type=jnp.float32
        )

    def multiply(c):
        for copy in weight_copies(c):
            copy.wait()
        plane_bulk(c).wait_recv()
        for b in range(4):
            part = pl.ds(b * block, block)
            rows = rows_in[c, part, :]
            gate_sum[part, :] += jnp.dot(rows, gate[c], preferred_element_type=jnp.float32)
            up_sum[part, :] += jnp.dot(rows, up[c], preferred_element_type=jnp.float32)

    def named(experts):
        hits = jnp.zeros((ids.shape[0], experts.shape[1]), jnp.float32)
        for k in range(TOP):
            hits += jnp.where(ids[:, k : k + 1] == experts, 1.0, 0.0)
        return hits

    def iota(shape, axis):
        return lax.broadcasted_iota(jnp.int32, shape, axis)

    line_start(0)
    line_start(1)
    group = ids.shape[0]
    ids_part = ids.at[pl.ds(0, (line - 1) * tokens)]
    ids_bulk = remote(ids_part, ids_part, ids_send, ids_recv, at.on_line(1)[1])
    ids_bulk.wait_recv()
    experts_here = homes_ref[...] + at.z * width
    hits = named(experts_here)
    before = jnp.where(iota((group, group), 1) < iota((group, group), 0), 1.0, 0.0)
    rank = jnp.dot(
        before.astype(jnp.bfloat16), hits.astype(jnp.bfloat16), preferred_element_type=jnp.float32
    )
    place = jnp.where(hits > 0.0, rank, -1.0).T
    seats = iota((cap, group), 0).astype(jnp.float32)
    for j in range(plane):
        seated = jnp.where(place[j : j + 1, :] == seats, 1.0, 0.0)
        pick[j * cap : (j + 1) * cap, :] = seated.astype(jnp.bfloat16)

    def step(c, carry):
        @pl.when(c + 2 < chunks)
        def _():
            line_start(c + 2)

        line_bulk(c).wait_recv()
        plane_start(c)

        @pl.when(c >= 1)
        def _():
            multiply(c - 1)

        return carry

    lax.fori_loop(0, chunks, step, 0)
    experts = logits.shape[1]
    masked = jnp.where(named(iota((1, experts), 1)) > 0.0, logits[...], -jnp.inf)
    raised = jnp.exp(masked - jnp.max(masked, axis=1, keepdims=True))
    weights = raised / jnp.sum(raised, axis=1, keepdims=True)
    select = jnp.where(iota((experts, experts_here.shape[1]), 0) == experts_here, 1.0, 0.0)
    weights_here = jnp.dot(
        weights.astype(jnp.bfloat16), select.astype(jnp.bfloat16),
        preferred_element_type=jnp.float32,
    ).T
    for j in range(plane):
        seat = pick[j * cap : (j + 1) * cap, :].astype(jnp.float32)
        mix_turned[j * cap : (j + 1) * cap, :] = weights_here[j : j + 1, :] * seat
    for b in range(total // 128):
        part = slice(b * 128, (b + 1) * 128)
        mix_ref[:, part] = mix_turned[part, :].T.astype(jnp.bfloat16)
    multiply(chunks - 1)
    for b in range(4):
        part = pl.ds(b * block, block)
        value = gate_sum[part, :]
        act_ref[part, :] = (value / (1.0 + jnp.exp(-value)) * up_sum[part, :]).astype(jnp.bfloat16)

    def drain(c, carry):
        line_bulk(c).wait_send()
        return carry

    lax.fori_loop(0, chunks, drain, 0)
    ids_bulk.wait_send()
    plane_bulk(chunks - 2).wait_send()
    plane_bulk(chunks - 1).wait_send()


def return_kernel(
    line, width, seq_count, cap,
    act_ref, mix_ref, hidden_ref, down_hbm,
    out_ref,
    down, made, rows_in, part_out, own_part, parts_in,
    plane_send, plane_recv, line_send, line_recv, weight_sem,
):
    at = Place(line, width, seq_count)
    chunks, _, cw = down.shape
    tokens = hidden_ref.shape[0]
    plane = at.plane
    total = plane * cap
    block = total // 4

    def weight_copy(c):
        return pltpu.make_async_copy(down_hbm.at[:, span(c, cw, cw)], down.at[c], weight_sem.at[c])

    def start_weights(c, carry):
        weight_copy(c).start()
        return carry

    lax.fori_loop(0, chunks, start_weights, 0)
    at.greet()

    def plane_bulk(c):
        part = pl.ds(0, (plane - 1) * cap)
        return remote(
            made.at[lax.rem(c, 2), part], rows_in.at[c, part],
            plane_send.at[c], plane_recv.at[c], at.in_plane(1)[1],
        )

    def line_bulk(c):
        return remote(
            part_out.at[lax.rem(c, 2)], parts_in.at[c],
            line_send.at[c], line_recv.at[c], at.on_line(1)[1],
        )

    def down_step(c):
        slot = lax.rem(c, 2)
        weight_copy(c).wait()

        @pl.when(c >= 2)
        def _():
            plane_bulk(c - 2).wait_send()

        for b in range(4):
            part = pl.ds(b * block, block)
            made[slot, part, :] = jnp.dot(
                act_ref[part, :], down[c], preferred_element_type=jnp.float32
            ).astype(jnp.bfloat16)
        mine = span(at.me, cap, 16)
        for k in range(1, plane):
            j, target = at.in_plane(k)
            remote(
                made.at[slot, span(j, cap, 16)], rows_in.at[c, mine],
                plane_send.at[c], plane_recv.at[c], target,
            ).start()
        rows_in[c, mine, :] = made[slot, mine, :]

    def merge_step(c):
        slot = lax.rem(c, 2)
        plane_bulk(c).wait_recv()

        @pl.when(c >= 2)
        def _():
            line_bulk(c - 2).wait_send()

        for k in range(1, line + 1):
            z, target = at.on_line(k)
            part = jnp.dot(
                mix_ref[span(z, tokens, tokens), :], rows_in[c],
                preferred_element_type=jnp.float32,
            )
            if k == line:
                own_part[slot] = part
            else:
                part_out[slot, k - 1] = part.astype(jnp.bfloat16)
                remote(
                    part_out.at[slot, k - 1], parts_in.at[c, k - 1],
                    line_send.at[c], line_recv.at[c], target,
                ).start()

    def finish_step(c):
        line_bulk(c).wait_recv()
        columns = span(c, cw, cw)
        value = hidden_ref[:, columns] + own_part[lax.rem(c, 2)]
        for k in range(line - 1):
            value += parts_in[c, k].astype(jnp.float32)
        out_ref[:, columns] = value.astype(jnp.bfloat16)

    def step(c, carry):
        @pl.when(c < chunks)
        def _():
            down_step(c)

        @pl.when((c >= 1) & (c <= chunks))
        def _():
            merge_step(c - 1)

        @pl.when(c >= 2)
        def _():
            finish_step(c - 2)

        return carry

    lax.fori_loop(0, chunks + 2, step, 0)
    for c in (chunks - 2, chunks - 1):
        plane_bulk(c).wait_send()
        line_bulk(c).wait_send()


def kernel_params(collective_id):
    return pltpu.CompilerParams(
        collective_id=collective_id, has_side_effects=True, vmem_limit_bytes=VMEM_BYTES
    )


def experts_layer(hidden_state, normed, router_weight, chosen_ids, w_gate, w_up, w_down):
    seq_count, exp_count = lax.axis_size("seq"), lax.axis_size("exp")
    tokens, width_d = normed.shape
    line, width = LINE, exp_count // LINE
    plane = seq_count * width
    experts = seq_count * exp_count
    hidden_units = w_gate.shape[1]
    per_block = max(2, (tokens * TOP * 9 + 8 * experts - 1) // (8 * experts))
    cap = (line * per_block + 15) // 16 * 16
    total = plane * cap
    group = line * tokens
    chunks = 16
    cw = width_d // chunks
    bf16, f32 = jnp.bfloat16, jnp.float32

    homes = np.full((1, 128), -experts, np.int32)
    homes[0, :plane] = [j // width * exp_count + j % width for j in range(plane)]

    vmem = pl.BlockSpec(memory_space=pltpu.VMEM)
    hbm = pl.BlockSpec(memory_space=pl.ANY)
    dma = pltpu.SemaphoreType.DMA
    act, mix = pl.pallas_call(
        functools.partial(dispatch_kernel, line, width, seq_count, cap),
        out_shape=(
            jax.ShapeDtypeStruct((total, hidden_units), bf16),
            jax.ShapeDtypeStruct((group, total), bf16),
        ),
        in_specs=[vmem, vmem, vmem, vmem, hbm, hbm],
        out_specs=(vmem, vmem),
        scratch_shapes=[
            pltpu.VMEM((group, TOP), jnp.int32),
            pltpu.VMEM((total, group), bf16),
            pltpu.VMEM((total, group), f32),
            pltpu.VMEM((group, experts), f32),
            pltpu.VMEM((chunks, group, cw), bf16),
            pltpu.VMEM((2, total, cw), bf16),
            pltpu.VMEM((chunks, total, cw), bf16),
            pltpu.VMEM((chunks, cw, hidden_units), bf16),
            pltpu.VMEM((chunks, cw, hidden_units), bf16),
            pltpu.VMEM((total, hidden_units), f32),
            pltpu.VMEM((total, hidden_units), f32),
            dma((chunks,)), dma((chunks,)), dma((chunks,)), dma((chunks,)), dma((2, chunks)),
            dma, dma,
        ],
        compiler_params=kernel_params(0),
        name="dispatch",
    )(normed, chosen_ids, jnp.asarray(homes), router_weight, w_gate, w_up)

    return pl.pallas_call(
        functools.partial(return_kernel, line, width, seq_count, cap),
        out_shape=jax.ShapeDtypeStruct((tokens, width_d), bf16),
        in_specs=[vmem, vmem, vmem, hbm],
        out_specs=vmem,
        scratch_shapes=[
            pltpu.VMEM((chunks, hidden_units, cw), bf16),
            pltpu.VMEM((2, total, cw), bf16),
            pltpu.VMEM((chunks, total, cw), bf16),
            pltpu.VMEM((2, line - 1, tokens, cw), bf16),
            pltpu.VMEM((2, tokens, cw), f32),
            pltpu.VMEM((chunks, line - 1, tokens, cw), bf16),
            dma((chunks,)), dma((chunks,)), dma((chunks,)), dma((chunks,)), dma((chunks,)),
        ],
        compiler_params=kernel_params(1),
        name="give_back",
    )(act, mix, hidden_state, w_down)


def attend_kernel(
    heads, group_length, prefix_total,
    queries_ref, keys_ref, values_ref, key_cache_ref, value_cache_ref, bias_ref, resid_ref,
    gain_ref, out_hbm,
    hidden_ref, normed_ref,
    query, key, value, mask, attended, weight, pair_out, pair_in, own_sum, far_out, far_in,
    key_send, key_recv, value_send, value_recv, query_send, query_recv,
    pair_send, pair_recv, far_send, far_recv, weight_sem,
):
    seq_count = lax.axis_size("seq")
    me = lax.axis_index("seq")
    core, chip = lax.rem(me, 2), lax.div(me, 2)
    partner = {"seq": 2 * chip + 1 - core}
    chips = seq_count // 2
    tokens = queries_ref.shape[0]
    cached = key_cache_ref.shape[1]
    chunks, _, cw = weight.shape
    bf16, f32 = jnp.bfloat16, jnp.float32

    def weight_copy(c):
        return pltpu.make_async_copy(out_hbm.at[:, span(c, cw, cw)], weight.at[c], weight_sem.at[c])

    def start_weights(c, carry):
        weight_copy(c).start()
        return carry

    lax.fori_loop(0, chunks, start_weights, 0)
    barrier = pltpu.get_barrier_semaphore()
    for k in range(1, seq_count):
        pl.semaphore_signal(
            barrier, inc=1, device_id={"seq": lax.rem(me + k, seq_count)}, device_id_type=MESH
        )
    pl.semaphore_wait(barrier, seq_count - 1)

    def head_of(peer):
        return lax.div(peer * heads, group_length)

    span_rows = pl.ds(pl.multiple_of(prefix_total + me * tokens, 16), tokens)
    cache_rows = span(me, cached, 16)
    own_rows = span(me, tokens, tokens)
    for k in range(1, seq_count):
        peer = lax.rem(me + k, seq_count)
        target = {"seq": peer}
        columns = span(head_of(peer), HEAD_SIZE, HEAD_SIZE)
        for new, cache, full, send, recv in (
            (keys_ref, key_cache_ref, key, key_send, key_recv),
            (values_ref, value_cache_ref, value, value_send, value_recv),
        ):
            remote(new.at[:, columns], full.at[span_rows], send, recv, target).start()
            remote(cache.at[head_of(peer)], full.at[cache_rows], send, recv, target).start()

    def start_queries(h, carry):
        for k in range(1, seq_count):
            peer = lax.rem(me + k, seq_count)
            remote(
                queries_ref.at[:, span(peer * heads + h, HEAD_SIZE, HEAD_SIZE)],
                query.at[h, own_rows], query_send.at[h], query_recv.at[h], {"seq": peer},
            ).start()
        query[h, own_rows, :] = queries_ref[:, span(me * heads + h, HEAD_SIZE, HEAD_SIZE)]
        return carry

    lax.fori_loop(0, heads, start_queries, 0)
    my_columns = span(head_of(me), HEAD_SIZE, HEAD_SIZE)
    key[span_rows, :] = keys_ref[:, my_columns]
    value[span_rows, :] = values_ref[:, my_columns]
    key[cache_rows, :] = key_cache_ref[head_of(me)]
    value[cache_rows, :] = value_cache_ref[head_of(me)]
    length = mask.shape[0]
    mask[:, :prefix_total] = jnp.broadcast_to(bias_ref[...], (length, prefix_total))
    later = lax.broadcasted_iota(jnp.int32, (length, length), 1) > lax.broadcasted_iota(
        jnp.int32, (length, length), 0
    )
    mask[:, prefix_total:] = jnp.where(later, -1e30, 0.0)

    def bulk(full, send, recv):
        part = full.at[pl.ds(0, (seq_count - 1) * (tokens + cached))]
        return remote(part, part, send, recv, {"seq": lax.rem(me + 1, seq_count)})

    key_bulk = bulk(key, key_send, key_recv)
    value_bulk = bulk(value, value_send, value_recv)
    key_bulk.wait_recv()
    value_bulk.wait_recv()

    def query_bulk(h):
        part = query.at[h, pl.ds(0, (seq_count - 1) * tokens)]
        return remote(
            part, part, query_send.at[h], query_recv.at[h], {"seq": lax.rem(me + 1, seq_count)}
        )

    def attend_head(h, carry):
        query_bulk(h).wait_recv()
        for b in range(seq_count):
            rows = slice(b * tokens, (b + 1) * tokens)
            reach = prefix_total + (b + 1) * tokens
            scores = lax.dot_general(
                query[h, rows, :], key[:reach, :], (((1,), (1,)), ((), ())),
                preferred_element_type=f32,
            ) * HEAD_SIZE ** (-0.5) + mask[rows, :reach]
            raised = jnp.exp(scores - jnp.max(scores, axis=1, keepdims=True))
            mixed = jnp.dot(raised.astype(bf16), value[:reach, :], preferred_element_type=f32)
            mixed = mixed / jnp.sum(raised, axis=1, keepdims=True)
            attended[rows, span(h, HEAD_SIZE, HEAD_SIZE)] = mixed.astype(bf16)
        return carry

    lax.fori_loop(0, heads, attend_head, 0)

    def pair_bulk(c):
        return remote(pair_out.at[c], pair_in.at[c], pair_send.at[c], pair_recv.at[c], partner)

    def far_bulk(c):
        return remote(far_out.at[c], far_in.at[c], far_send.at[c], far_recv.at[c], partner)

    def project(c, owner):
        rows = span(owner, tokens, tokens)
        return jnp.dot(attended[rows, :], weight[c], preferred_element_type=f32)

    def pair_step(c):
        weight_copy(c).wait()
        for k in range(chips):
            there = lax.rem(chip + k, chips)
            pair_out[c, k] = project(c, 2 * there + 1 - core).astype(bf16)
        pair_bulk(c).start()
        for k in range(chips):
            there = lax.rem(chip + k, chips)
            own_sum[lax.rem(c, 2), k] = project(c, 2 * there + core)

    def far_step(c):
        pair_bulk(c).wait_recv()
        for k in range(1, chips):
            there = lax.rem(chip + k, chips)
            both = own_sum[lax.rem(c, 2), k] + pair_in[c, k].astype(f32)
            far_out[c, k - 1] = both.astype(bf16)
            remote(
                far_out.at[c, k - 1], far_in.at[c, k - 1], far_send.at[c], far_recv.at[c],
                {"seq": 2 * there + core},
            ).start()
        columns = span(c, cw, cw)
        hidden_ref[:, columns] = (
            resid_ref[:, columns].astype(f32) + own_sum[lax.rem(c, 2), 0] + pair_in[c, 0].astype(f32)
        )

    def step(c, carry):
        @pl.when(c < chunks)
        def _():
            pair_step(c)

        @pl.when(c >= 1)
        def _():
            far_step(c - 1)

        return carry

    lax.fori_loop(0, chunks + 1, step, 0)

    def sum_step(c, square):
        far_bulk(c).wait_recv()
        columns = span(c, cw, cw)
        total = hidden_ref[:, columns]
        for k in range(chips - 1):
            total += far_in[c, k].astype(f32)
        hidden_ref[:, columns] = total
        return square + jnp.sum(total * total, axis=1, keepdims=True)

    square = lax.fori_loop(0, chunks, sum_step, jnp.zeros((tokens, 1), f32))
    factor = lax.rsqrt(square / hidden_ref.shape[1] + 1e-06)
    for c in range(chunks):
        columns = slice(c * cw, (c + 1) * cw)
        normed_ref[:, columns] = (hidden_ref[:, columns] * factor * gain_ref[:, columns]).astype(bf16)

    key_bulk.wait_send()
    value_bulk.wait_send()

    def drain_queries(h, carry):
        query_bulk(h).wait_send()
        return carry

    def drain(c, carry):
        pair_bulk(c).wait_send()
        far_bulk(c).wait_send()
        return carry

    lax.fori_loop(0, heads, drain_queries, 0)
    lax.fori_loop(0, chunks, drain, 0)


def per_device(
    resid,
    queries,
    span_rotated_keys,
    span_value_rows,
    key_cache,
    prefix_value_cache,
    prefix_len,
    out_weight,
    norm_gain,
    router_weight,
    expert_ids,
    w_gate,
    w_up,
    w_down,
):
    seq_count = lax.axis_size("seq")
    tokens, model_width = resid.shape[1:]
    heads = QUERY_HEAD_HALF // seq_count
    group_length = QUERY_HEAD_HALF // KEY_VALUE_HEADS
    prefix_total = key_cache.shape[2] * seq_count
    length = tokens * seq_count
    chips = seq_count // 2
    chunks = 8
    cw = model_width // chunks
    bf16, f32 = jnp.bfloat16, jnp.float32
    live = jnp.arange(prefix_total, dtype=jnp.int32) < prefix_len[0]
    bias = jnp.where(live, 0.0, -1e30).astype(f32)[None]

    vmem = pl.BlockSpec(memory_space=pltpu.VMEM)
    hbm = pl.BlockSpec(memory_space=pl.ANY)
    dma = pltpu.SemaphoreType.DMA
    hidden_state, normed = pl.pallas_call(
        functools.partial(attend_kernel, heads, group_length, prefix_total),
        out_shape=(
            jax.ShapeDtypeStruct((tokens, model_width), f32),
            jax.ShapeDtypeStruct((tokens, model_width), bf16),
        ),
        in_specs=[vmem] * 8 + [hbm],
        out_specs=(vmem, vmem),
        scratch_shapes=[
            pltpu.VMEM((heads, length, HEAD_SIZE), bf16),
            pltpu.VMEM((prefix_total + length, HEAD_SIZE), bf16),
            pltpu.VMEM((prefix_total + length, HEAD_SIZE), bf16),
            pltpu.VMEM((length, prefix_total + length), f32),
            pltpu.VMEM((length, heads * HEAD_SIZE), bf16),
            pltpu.VMEM((chunks, heads * HEAD_SIZE, cw), bf16),
            pltpu.VMEM((chunks, chips, tokens, cw), bf16),
            pltpu.VMEM((chunks, chips, tokens, cw), bf16),
            pltpu.VMEM((2, chips, tokens, cw), f32),
            pltpu.VMEM((chunks, chips - 1, tokens, cw), bf16),
            pltpu.VMEM((chunks, chips - 1, tokens, cw), bf16),
            dma, dma, dma, dma, dma((heads,)), dma((heads,)),
            dma((chunks,)), dma((chunks,)), dma((chunks,)), dma((chunks,)), dma((chunks,)),
        ],
        compiler_params=kernel_params(2),
        name="attend",
    )(
        queries[0], span_rotated_keys[0], span_value_rows[0], key_cache[0],
        prefix_value_cache[0], bias, resid[0], norm_gain[None], out_weight,
    )
    out = experts_layer(
        hidden_state, normed, router_weight, expert_ids[0], w_gate[0], w_up[0], w_down[0]
    )
    return out[None]


def solution(mesh):
    in_specs = (
        P("exp", "seq", None),
        P("exp", "seq", None),
        P("exp", "seq", None),
        P("exp", "seq", None),
        P("exp", None, "seq", None),
        P("exp", None, "seq", None),
        P("exp"),
        P("seq", None),
        P(),
        P(),
        P("exp", "seq", None),
        P(("seq", "exp"), None, None),
        P(("seq", "exp"), None, None),
        P(("seq", "exp"), None, None),
    )
    out_specs = P("exp", "seq", None)
    return jax.shard_map(
        per_device, mesh=mesh, in_specs=in_specs, out_specs=out_specs, check_vma=False
    )
```

```python
import functools

import jax
import jax.numpy as jnp
import numpy as np
from jax import lax
from jax.experimental import pallas as pl
from jax.experimental.pallas import tpu as pltpu
from jax.sharding import PartitionSpec as P

QUERY_HEAD_HALF = 32
KEY_VALUE_HEADS = 4
HEAD_SIZE = 128
TOP = 8


LINE = 4
MESH = pl.DeviceIdType.MESH
VMEM_BYTES = 60 * 1024 * 1024


class Place:
    def __init__(self, line, width, seq_count):
        self.line, self.width, self.plane = line, width, width * seq_count
        self.seq, exp = lax.axis_index("seq"), lax.axis_index("exp")
        self.z, self.x = lax.div(exp, width), lax.rem(exp, width)
        self.me = self.seq * width + self.x

    def on_line(self, k):
        z = lax.rem(self.z + k, self.line)
        return z, {"seq": self.seq, "exp": z * self.width + self.x}

    def in_plane(self, k):
        core, chip = lax.rem(self.seq, 2), lax.div(self.seq, 2)
        chips = self.plane // self.width // 2
        steps = [(b, c, a) for a in range(2) for b in range(self.width) for c in range(chips)]
        near = [step for step in steps if step[0] == 0 and step[1] == 0]
        far = [step for step in steps if step[0] or step[1]]
        far.sort(key=lambda step: (step[2], step[0] > 0 and step[1] > 0))
        dx, dy, dc = (near[:1] + far + near[1:])[k]
        seq = 2 * lax.rem(chip + dy, chips) + lax.rem(core + dc, 2)
        x = lax.rem(self.x + dx, self.width)
        return seq * self.width + x, {"seq": seq, "exp": self.z * self.width + x}

    def greet(self):
        barrier = pltpu.get_barrier_semaphore()
        for k in range(1, self.line):
            pl.semaphore_signal(
                barrier, inc=1, device_id=self.on_line(k)[1], device_id_type=MESH
            )
        for k in range(1, self.plane):
            pl.semaphore_signal(
                barrier, inc=1, device_id=self.in_plane(k)[1], device_id_type=MESH
            )
        pl.semaphore_wait(barrier, self.line + self.plane - 2)


def span(start, size, step):
    return pl.ds(pl.multiple_of(start * size, step), size)


def remote(src, dst, send, recv, target):
    return pltpu.make_async_remote_copy(
        src_ref=src, dst_ref=dst, send_sem=send, recv_sem=recv,
        device_id=target, device_id_type=MESH,
    )


def dispatch_kernel(
    line, width, seq_count, cap,
    normed_ref, ids_ref, homes_ref, router_ref, gate_hbm, up_hbm,
    act_ref, mix_ref,
    ids, pick, mix_turned, logits, lines, pack, rows_in, gate, up, gate_sum, up_sum,
    line_send, line_recv, plane_send, plane_recv, weight_sem, ids_send, ids_recv,
):
    at = Place(line, width, seq_count)
    chunks, _, cw = lines.shape
    tokens = normed_ref.shape[0]
    plane = at.plane
    total = plane * cap
    block = total // 4

    def weight_copies(c):
        return (
            pltpu.make_async_copy(gate_hbm.at[span(c, cw, cw)], gate.at[c], weight_sem.at[0, c]),
            pltpu.make_async_copy(up_hbm.at[span(c, cw, cw)], up.at[c], weight_sem.at[1, c]),
        )

    def start_weights(c, carry):
        for copy in weight_copies(c):
            copy.start()
        return carry

    lax.fori_loop(0, chunks, start_weights, 0)
    own = span(at.z, tokens, tokens)
    at.greet()
    ids[at.z] = ids_ref[...]
    for k in range(1, line):
        remote(ids.at[at.z], ids.at[at.z], ids_send, ids_recv, at.on_line(k)[1]).start()

    def line_start(c):
        for k in range(1, line):
            target = at.on_line(k)[1]
            part = lines.at[c, own]
            remote(part, part, line_send.at[c], line_recv.at[c], target).start()

    def line_bulk(c):
        part = lines.at[c, pl.ds(0, (line - 1) * tokens)]
        return remote(part, part, line_send.at[c], line_recv.at[c], at.on_line(1)[1])

    def plane_bulk(c):
        part = pl.ds(0, (plane - 1) * cap)
        return remote(
            pack.at[lax.rem(c, 2), part], rows_in.at[c, part],
            plane_send.at[c], plane_recv.at[c], at.in_plane(1)[1],
        )

    def plane_start(c):
        slot = lax.rem(c, 2)

        @pl.when(c >= 2)
        def _():
            plane_bulk(c - 2).wait_send()

        for b in range(4):
            part = pl.ds(b * block, block)
            pack[slot, part, :] = jnp.dot(
                pick[part, :], lines[c], preferred_element_type=jnp.float32
            ).astype(jnp.bfloat16)
        mine = span(at.me, cap, 16)
        for k in range(1, plane):
            j, target = at.in_plane(k)
            remote(
                pack.at[slot, span(j, cap, 16)], rows_in.at[c, mine],
                plane_send.at[c], plane_recv.at[c], target,
            ).start()
        rows_in[c, mine, :] = pack[slot, mine, :]
        logits[...] += lax.dot_general(
            router_ref[:, span(c, cw, cw)], lines[c], (((1,), (1,)), ((), ())),
            preferred_element_type=jnp.float32,
        )

    def multiply(c):
        for copy in weight_copies(c):
            copy.wait()
        plane_bulk(c).wait_recv()
        for b in range(4):
            part = pl.ds(b * block, block)
            rows = rows_in[c, part, :]
            gate_sum[part, :] += jnp.dot(rows, gate[c], preferred_element_type=jnp.float32)
            up_sum[part, :] += jnp.dot(rows, up[c], preferred_element_type=jnp.float32)

    def iota(shape, axis):
        return lax.broadcasted_iota(jnp.int32, shape, axis)

    def named(experts):
        blocks = []
        for z in range(line):
            hits = jnp.zeros((experts.shape[0], tokens), jnp.float32)
            for k in range(TOP):
                hits += jnp.where(ids[z, k : k + 1, :] == experts, 1.0, 0.0)
            blocks.append(hits)
        return jnp.concatenate(blocks, axis=1)

    for c in range(chunks):
        lines[c, own, :] = normed_ref[:, c * cw : (c + 1) * cw]
        if c < 2:
            line_start(c)
    group = line * tokens
    ids_part = ids.at[pl.ds(0, line - 1)]
    ids_bulk = remote(ids_part, ids_part, ids_send, ids_recv, at.on_line(1)[1])
    ids_bulk.wait_recv()
    experts_here = homes_ref[...] + at.z * width
    hits = named(experts_here)
    before = jnp.where(iota((group, group), 0) < iota((group, group), 1), 1.0, 0.0)
    rank = jnp.dot(
        hits.astype(jnp.bfloat16), before.astype(jnp.bfloat16), preferred_element_type=jnp.float32
    )
    place = jnp.where(hits > 0.0, rank, -1.0)
    seats = iota((cap, group), 0).astype(jnp.float32)
    for j in range(plane):
        seated = jnp.where(place[j : j + 1, :] == seats, 1.0, 0.0)
        pick[j * cap : (j + 1) * cap, :] = seated.astype(jnp.bfloat16)
    logits[...] = jnp.zeros_like(logits)
    gate_sum[...] = jnp.zeros_like(gate_sum)
    up_sum[...] = jnp.zeros_like(up_sum)

    def step(c, carry):
        @pl.when(c + 2 < chunks)
        def _():
            line_start(c + 2)

        line_bulk(c).wait_recv()
        plane_start(c)

        @pl.when(c >= 1)
        def _():
            multiply(c - 1)

        return carry

    lax.fori_loop(0, chunks, step, 0)
    experts = logits.shape[0]
    masked = jnp.where(named(iota((experts, 1), 0)) > 0.0, logits[...], -jnp.inf)
    raised = jnp.exp(masked - jnp.max(masked, axis=0, keepdims=True))
    weights = raised / jnp.sum(raised, axis=0, keepdims=True)
    select = jnp.where(iota((experts_here.shape[0], experts), 1) == experts_here, 1.0, 0.0)
    weights_here = jnp.dot(
        select.astype(jnp.bfloat16), weights.astype(jnp.bfloat16),
        preferred_element_type=jnp.float32,
    )
    for j in range(plane):
        seat = pick[j * cap : (j + 1) * cap, :].astype(jnp.float32)
        mix_turned[j * cap : (j + 1) * cap, :] = weights_here[j : j + 1, :] * seat
    for b in range(total // 128):
        part = slice(b * 128, (b + 1) * 128)
        mix_ref[:, part] = mix_turned[part, :].T.astype(jnp.bfloat16)
    multiply(chunks - 1)
    for b in range(4):
        part = pl.ds(b * block, block)
        value = gate_sum[part, :]
        act_ref[part, :] = (value / (1.0 + jnp.exp(-value)) * up_sum[part, :]).astype(jnp.bfloat16)

    def drain(c, carry):
        line_bulk(c).wait_send()
        return carry

    lax.fori_loop(0, chunks, drain, 0)
    ids_bulk.wait_send()
    plane_bulk(chunks - 2).wait_send()
    plane_bulk(chunks - 1).wait_send()


def return_kernel(
    line, width, seq_count, cap,
    act_ref, mix_ref, hidden_ref, down_hbm,
    out_ref,
    down, made, rows_in, part_out, own_part, parts_in,
    plane_send, plane_recv, line_send, line_recv, weight_sem,
):
    at = Place(line, width, seq_count)
    chunks, _, cw = down.shape
    tokens = hidden_ref.shape[0]
    plane = at.plane
    total = plane * cap
    block = total // 4

    def weight_copy(c):
        return pltpu.make_async_copy(down_hbm.at[:, span(c, cw, cw)], down.at[c], weight_sem.at[c])

    def start_weights(c, carry):
        weight_copy(c).start()
        return carry

    lax.fori_loop(0, chunks, start_weights, 0)
    at.greet()

    def plane_bulk(c):
        part = pl.ds(0, (plane - 1) * cap)
        return remote(
            made.at[lax.rem(c, 2), part], rows_in.at[c, part],
            plane_send.at[c], plane_recv.at[c], at.in_plane(1)[1],
        )

    def line_bulk(c):
        return remote(
            part_out.at[lax.rem(c, 2)], parts_in.at[c],
            line_send.at[c], line_recv.at[c], at.on_line(1)[1],
        )

    def down_step(c):
        slot = lax.rem(c, 2)
        weight_copy(c).wait()

        @pl.when(c >= 2)
        def _():
            plane_bulk(c - 2).wait_send()

        for b in range(4):
            part = pl.ds(b * block, block)
            made[slot, part, :] = jnp.dot(
                act_ref[part, :], down[c], preferred_element_type=jnp.float32
            ).astype(jnp.bfloat16)
        mine = span(at.me, cap, 16)
        for k in range(1, plane):
            j, target = at.in_plane(k)
            remote(
                made.at[slot, span(j, cap, 16)], rows_in.at[c, mine],
                plane_send.at[c], plane_recv.at[c], target,
            ).start()
        rows_in[c, mine, :] = made[slot, mine, :]

    def merge_step(c):
        slot = lax.rem(c, 2)
        plane_bulk(c).wait_recv()

        @pl.when(c >= 2)
        def _():
            line_bulk(c - 2).wait_send()

        for k in range(1, line + 1):
            z, target = at.on_line(k)
            part = jnp.dot(
                mix_ref[span(z, tokens, tokens), :], rows_in[c],
                preferred_element_type=jnp.float32,
            )
            if k == line:
                own_part[slot] = part
            else:
                part_out[slot, k - 1] = part.astype(jnp.bfloat16)
                remote(
                    part_out.at[slot, k - 1], parts_in.at[c, k - 1],
                    line_send.at[c], line_recv.at[c], target,
                ).start()

    def finish_step(c):
        line_bulk(c).wait_recv()
        columns = span(c, cw, cw)
        value = hidden_ref[:, columns] + own_part[lax.rem(c, 2)]
        for k in range(line - 1):
            value += parts_in[c, k].astype(jnp.float32)
        out_ref[:, columns] = value.astype(jnp.bfloat16)

    def step(c, carry):
        @pl.when(c < chunks)
        def _():
            down_step(c)

        @pl.when((c >= 1) & (c <= chunks))
        def _():
            merge_step(c - 1)

        @pl.when(c >= 2)
        def _():
            finish_step(c - 2)

        return carry

    lax.fori_loop(0, chunks + 2, step, 0)
    for c in (chunks - 2, chunks - 1):
        plane_bulk(c).wait_send()
        line_bulk(c).wait_send()


def kernel_params(collective_id):
    return pltpu.CompilerParams(
        collective_id=collective_id, has_side_effects=True, vmem_limit_bytes=VMEM_BYTES
    )


def experts_layer(hidden_state, normed, router_weight, chosen_ids, w_gate, w_up, w_down):
    seq_count, exp_count = lax.axis_size("seq"), lax.axis_size("exp")
    tokens, width_d = normed.shape
    line, width = LINE, exp_count // LINE
    plane = seq_count * width
    experts = seq_count * exp_count
    hidden_units = w_gate.shape[1]
    per_block = max(2, (tokens * TOP * 9 + 8 * experts - 1) // (8 * experts))
    cap = (line * per_block + 15) // 16 * 16
    total = plane * cap
    group = line * tokens
    chunks = 16
    cw = width_d // chunks
    bf16, f32 = jnp.bfloat16, jnp.float32

    homes = np.full((128, 1), -experts, np.int32)
    homes[:plane, 0] = [j // width * exp_count + j % width for j in range(plane)]

    vmem = pl.BlockSpec(memory_space=pltpu.VMEM)
    hbm = pl.BlockSpec(memory_space=pl.ANY)
    dma = pltpu.SemaphoreType.DMA
    act, mix = pl.pallas_call(
        functools.partial(dispatch_kernel, line, width, seq_count, cap),
        out_shape=(
            jax.ShapeDtypeStruct((total, hidden_units), bf16),
            jax.ShapeDtypeStruct((group, total), bf16),
        ),
        in_specs=[vmem, vmem, vmem, vmem, hbm, hbm],
        out_specs=(vmem, vmem),
        scratch_shapes=[
            pltpu.VMEM((line, TOP, tokens), jnp.int32),
            pltpu.VMEM((total, group), bf16),
            pltpu.VMEM((total, group), f32),
            pltpu.VMEM((experts, group), f32),
            pltpu.VMEM((chunks, group, cw), bf16),
            pltpu.VMEM((2, total, cw), bf16),
            pltpu.VMEM((chunks, total, cw), bf16),
            pltpu.VMEM((chunks, cw, hidden_units), bf16),
            pltpu.VMEM((chunks, cw, hidden_units), bf16),
            pltpu.VMEM((total, hidden_units), f32),
            pltpu.VMEM((total, hidden_units), f32),
            dma((chunks,)), dma((chunks,)), dma((chunks,)), dma((chunks,)), dma((2, chunks)),
            dma, dma,
        ],
        compiler_params=kernel_params(0),
        name="dispatch",
    )(normed, chosen_ids.T, jnp.asarray(homes), router_weight.T, w_gate, w_up)

    return pl.pallas_call(
        functools.partial(return_kernel, line, width, seq_count, cap),
        out_shape=jax.ShapeDtypeStruct((tokens, width_d), bf16),
        in_specs=[vmem, vmem, vmem, hbm],
        out_specs=vmem,
        scratch_shapes=[
            pltpu.VMEM((chunks, hidden_units, cw), bf16),
            pltpu.VMEM((2, total, cw), bf16),
            pltpu.VMEM((chunks, total, cw), bf16),
            pltpu.VMEM((2, line - 1, tokens, cw), bf16),
            pltpu.VMEM((2, tokens, cw), f32),
            pltpu.VMEM((chunks, line - 1, tokens, cw), bf16),
            dma((chunks,)), dma((chunks,)), dma((chunks,)), dma((chunks,)), dma((chunks,)),
        ],
        compiler_params=kernel_params(1),
        name="give_back",
    )(act, mix, hidden_state, w_down)


def attend_kernel(
    heads, group_length, prefix_total,
    queries_ref, keys_ref, values_ref, key_cache_ref, value_cache_ref, bias_ref, resid_ref,
    gain_ref, out_hbm,
    hidden_ref, normed_ref,
    query, key, value, mask, attended, weight, pair_out, pair_in, own_sum, far_out, far_in,
    key_send, key_recv, value_send, value_recv, query_send, query_recv,
    pair_send, pair_recv, far_send, far_recv, weight_sem,
):
    seq_count = lax.axis_size("seq")
    me = lax.axis_index("seq")
    core, chip = lax.rem(me, 2), lax.div(me, 2)
    partner = {"seq": 2 * chip + 1 - core}
    chips = seq_count // 2
    tokens = queries_ref.shape[0]
    cached = key_cache_ref.shape[1]
    chunks, _, cw = weight.shape
    bf16, f32 = jnp.bfloat16, jnp.float32

    def weight_copy(c):
        return pltpu.make_async_copy(out_hbm.at[:, span(c, cw, cw)], weight.at[c], weight_sem.at[c])

    def start_weights(c, carry):
        weight_copy(c).start()
        return carry

    lax.fori_loop(0, chunks, start_weights, 0)
    barrier = pltpu.get_barrier_semaphore()
    for k in range(1, seq_count):
        pl.semaphore_signal(
            barrier, inc=1, device_id={"seq": lax.rem(me + k, seq_count)}, device_id_type=MESH
        )
    pl.semaphore_wait(barrier, seq_count - 1)

    def head_of(peer):
        return lax.div(peer * heads, group_length)

    span_rows = pl.ds(pl.multiple_of(prefix_total + me * tokens, 16), tokens)
    cache_rows = span(me, cached, 16)
    own_rows = span(me, tokens, tokens)
    for k in range(1, seq_count):
        peer = lax.rem(me + k, seq_count)
        target = {"seq": peer}
        columns = span(head_of(peer), HEAD_SIZE, HEAD_SIZE)
        for new, cache, full, send, recv in (
            (keys_ref, key_cache_ref, key, key_send, key_recv),
            (values_ref, value_cache_ref, value, value_send, value_recv),
        ):
            remote(new.at[:, columns], full.at[span_rows], send, recv, target).start()
            remote(cache.at[head_of(peer)], full.at[cache_rows], send, recv, target).start()

    def start_queries(h, carry):
        for k in range(1, seq_count):
            peer = lax.rem(me + k, seq_count)
            remote(
                queries_ref.at[:, span(peer * heads + h, HEAD_SIZE, HEAD_SIZE)],
                query.at[h, own_rows], query_send.at[h], query_recv.at[h], {"seq": peer},
            ).start()
        query[h, own_rows, :] = queries_ref[:, span(me * heads + h, HEAD_SIZE, HEAD_SIZE)]
        return carry

    lax.fori_loop(0, heads, start_queries, 0)
    my_columns = span(head_of(me), HEAD_SIZE, HEAD_SIZE)
    key[span_rows, :] = keys_ref[:, my_columns]
    value[span_rows, :] = values_ref[:, my_columns]
    key[cache_rows, :] = key_cache_ref[head_of(me)]
    value[cache_rows, :] = value_cache_ref[head_of(me)]
    length = mask.shape[0]
    mask[:, :prefix_total] = jnp.broadcast_to(bias_ref[...], (length, prefix_total))
    later = lax.broadcasted_iota(jnp.int32, (length, length), 1) > lax.broadcasted_iota(
        jnp.int32, (length, length), 0
    )
    mask[:, prefix_total:] = jnp.where(later, -1e30, 0.0)

    def bulk(full, send, recv):
        part = full.at[pl.ds(0, (seq_count - 1) * (tokens + cached))]
        return remote(part, part, send, recv, {"seq": lax.rem(me + 1, seq_count)})

    key_bulk = bulk(key, key_send, key_recv)
    value_bulk = bulk(value, value_send, value_recv)
    key_bulk.wait_recv()
    value_bulk.wait_recv()

    def query_bulk(h):
        part = query.at[h, pl.ds(0, (seq_count - 1) * tokens)]
        return remote(
            part, part, query_send.at[h], query_recv.at[h], {"seq": lax.rem(me + 1, seq_count)}
        )

    def attend_block(h, b):
        rows = slice(b * tokens, (b + 1) * tokens)
        reach = prefix_total + (b + 1) * tokens
        scores = lax.dot_general(
            query[h, rows, :], key[:reach, :], (((1,), (1,)), ((), ())),
            preferred_element_type=f32,
        ) * HEAD_SIZE ** (-0.5) + mask[rows, :reach]
        raised = jnp.exp(scores - jnp.max(scores, axis=1, keepdims=True))
        mixed = jnp.dot(raised.astype(bf16), value[:reach, :], preferred_element_type=f32)
        mixed = mixed / jnp.sum(raised, axis=1, keepdims=True)
        attended[rows, span(h, HEAD_SIZE, HEAD_SIZE)] = mixed.astype(bf16)

    def far_head(h, carry):
        query_bulk(h).wait_recv()
        for y in range(chips):

            @pl.when(chip != y)
            def _():
                attend_block(h, 2 * y)
                attend_block(h, 2 * y + 1)

        return carry

    def near_head(h, carry):
        for y in range(chips):

            @pl.when(chip == y)
            def _():
                attend_block(h, 2 * y)
                attend_block(h, 2 * y + 1)

        return carry

    def pair_bulk(c):
        return remote(
            pair_out.at[c, pl.ds(1, chips - 1)], pair_in.at[c, pl.ds(1, chips - 1)],
            pair_send.at[0, c], pair_recv.at[0, c], partner,
        )

    def near_bulk(c):
        return remote(
            pair_out.at[c, 0], pair_in.at[c, 0], pair_send.at[1, c], pair_recv.at[1, c], partner
        )

    def far_bulk(c):
        return remote(far_out.at[c], far_in.at[c], far_send.at[c], far_recv.at[c], partner)

    def project(c, owner):
        rows = span(owner, tokens, tokens)
        return jnp.dot(attended[rows, :], weight[c], preferred_element_type=f32)

    def pair_step(c):
        weight_copy(c).wait()
        for k in range(1, chips):
            there = lax.rem(chip + k, chips)
            pair_out[c, k] = project(c, 2 * there + 1 - core).astype(bf16)
        pair_bulk(c).start()
        for k in range(1, chips):
            there = lax.rem(chip + k, chips)
            own_sum[lax.rem(c, 2), k - 1] = project(c, 2 * there + core)

    def far_step(c):
        pair_bulk(c).wait_recv()
        for k in range(1, chips):
            there = lax.rem(chip + k, chips)
            both = own_sum[lax.rem(c, 2), k - 1] + pair_in[c, k].astype(f32)
            far_out[c, k - 1] = both.astype(bf16)
            remote(
                far_out.at[c, k - 1], far_in.at[c, k - 1], far_send.at[c], far_recv.at[c],
                {"seq": 2 * there + core},
            ).start()

    def step(c, carry):
        @pl.when(c < chunks)
        def _():
            pair_step(c)

        @pl.when(c >= 1)
        def _():
            far_step(c - 1)

        return carry

    def near_step(c, carry):
        pair_out[c, 0] = project(c, 2 * chip + 1 - core).astype(bf16)
        near_bulk(c).start()
        columns = span(c, cw, cw)
        hidden_ref[:, columns] = resid_ref[:, columns].astype(f32) + project(c, me)
        return carry

    lax.fori_loop(0, heads, far_head, 0)
    lax.fori_loop(0, chunks + 1, step, 0)
    lax.fori_loop(0, heads, near_head, 0)
    lax.fori_loop(0, chunks, near_step, 0)

    def sum_step(c, square):
        near_bulk(c).wait_recv()
        far_bulk(c).wait_recv()
        columns = span(c, cw, cw)
        total = hidden_ref[:, columns] + pair_in[c, 0].astype(f32)
        for k in range(chips - 1):
            total += far_in[c, k].astype(f32)
        hidden_ref[:, columns] = total
        return square + jnp.sum(total * total, axis=1, keepdims=True)

    square = lax.fori_loop(0, chunks, sum_step, jnp.zeros((tokens, 1), f32))
    factor = lax.rsqrt(square / hidden_ref.shape[1] + 1e-06)
    for c in range(chunks):
        columns = slice(c * cw, (c + 1) * cw)
        normed_ref[:, columns] = (hidden_ref[:, columns] * factor * gain_ref[:, columns]).astype(bf16)

    key_bulk.wait_send()
    value_bulk.wait_send()

    def drain_queries(h, carry):
        query_bulk(h).wait_send()
        return carry

    def drain(c, carry):
        pair_bulk(c).wait_send()
        near_bulk(c).wait_send()
        far_bulk(c).wait_send()
        return carry

    lax.fori_loop(0, heads, drain_queries, 0)
    lax.fori_loop(0, chunks, drain, 0)


def per_device(
    resid,
    queries,
    span_rotated_keys,
    span_value_rows,
    key_cache,
    prefix_value_cache,
    prefix_len,
    out_weight,
    norm_gain,
    router_weight,
    expert_ids,
    w_gate,
    w_up,
    w_down,
):
    seq_count = lax.axis_size("seq")
    tokens, model_width = resid.shape[1:]
    heads = QUERY_HEAD_HALF // seq_count
    group_length = QUERY_HEAD_HALF // KEY_VALUE_HEADS
    prefix_total = key_cache.shape[2] * seq_count
    length = tokens * seq_count
    chips = seq_count // 2
    chunks = 8
    cw = model_width // chunks
    bf16, f32 = jnp.bfloat16, jnp.float32
    live = jnp.arange(prefix_total, dtype=jnp.int32) < prefix_len[0]
    bias = jnp.where(live, 0.0, -1e30).astype(f32)[None]

    vmem = pl.BlockSpec(memory_space=pltpu.VMEM)
    hbm = pl.BlockSpec(memory_space=pl.ANY)
    dma = pltpu.SemaphoreType.DMA
    hidden_state, normed = pl.pallas_call(
        functools.partial(attend_kernel, heads, group_length, prefix_total),
        out_shape=(
            jax.ShapeDtypeStruct((tokens, model_width), f32),
            jax.ShapeDtypeStruct((tokens, model_width), bf16),
        ),
        in_specs=[vmem] * 8 + [hbm],
        out_specs=(vmem, vmem),
        scratch_shapes=[
            pltpu.VMEM((heads, length, HEAD_SIZE), bf16),
            pltpu.VMEM((prefix_total + length, HEAD_SIZE), bf16),
            pltpu.VMEM((prefix_total + length, HEAD_SIZE), bf16),
            pltpu.VMEM((length, prefix_total + length), f32),
            pltpu.VMEM((length, heads * HEAD_SIZE), bf16),
            pltpu.VMEM((chunks, heads * HEAD_SIZE, cw), bf16),
            pltpu.VMEM((chunks, chips, tokens, cw), bf16),
            pltpu.VMEM((chunks, chips, tokens, cw), bf16),
            pltpu.VMEM((2, chips - 1, tokens, cw), f32),
            pltpu.VMEM((chunks, chips - 1, tokens, cw), bf16),
            pltpu.VMEM((chunks, chips - 1, tokens, cw), bf16),
            dma, dma, dma, dma, dma((heads,)), dma((heads,)),
            dma((2, chunks)), dma((2, chunks)), dma((chunks,)), dma((chunks,)), dma((chunks,)),
        ],
        compiler_params=kernel_params(2),
        name="attend",
    )(
        queries[0], span_rotated_keys[0], span_value_rows[0], key_cache[0],
        prefix_value_cache[0], bias, resid[0], norm_gain[None], out_weight,
    )
    out = experts_layer(
        hidden_state, normed, router_weight, expert_ids[0], w_gate[0], w_up[0], w_down[0]
    )
    return out[None]


def solution(mesh):
    in_specs = (
        P("exp", "seq", None),
        P("exp", "seq", None),
        P("exp", "seq", None),
        P("exp", "seq", None),
        P("exp", None, "seq", None),
        P("exp", None, "seq", None),
        P("exp"),
        P("seq", None),
        P(),
        P(),
        P("exp", "seq", None),
        P(("seq", "exp"), None, None),
        P(("seq", "exp"), None, None),
        P(("seq", "exp"), None, None),
    )
    out_specs = P("exp", "seq", None)
    return jax.shard_map(
        per_device, mesh=mesh, in_specs=in_specs, out_specs=out_specs, check_vma=False
    )
```
